256 devices in a mesh: tracer: 4 (over x_hi, core), cols: 64 (over z, y, x_lo).
Axes of the slice: x: 4 (x_hi: 2, x_lo: 2; x = x_hi * 2 + x_lo), y: 4, z: 8, core: 2. Of those that a mesh axis runs over, the one named last changes fastest.
Arguments:
- tracers: float32 [256, 4, 512, 128], P('tracer', None, 'cols'), may hold values from 0.2 to 5
- air_mass: float32 [4, 512, 128], P(None, 'cols'), may hold values from 1.5 to 3
- wind_x: float32 [2, 4, 512, 128], P(None, 'tracer', 'cols'), may hold values from -1 to 1
- wind_y: float32 [2, 4, 512, 128], P(None, 'tracer', 'cols'), may hold values from -1 to 1
- spacing_x: float32 [512, 128], P('cols'), may hold values from 0.5 to 1
- spacing_y: float32 [512, 128], P('cols'), may hold values from 0.5 to 1
- edge_mass_x: float32 [4, 512, 128], P('tracer', 'cols'), may hold values from 0.3 to 1
- edge_mass_y: float32 [4, 512, 128], P('tracer', 'cols'), may hold values from 0.3 to 1
Outputs:
- mixing: float32 [256, 4, 512, 128], P('tracer', None, 'cols')
The draws below stay inside these ranges and needn't reach their ends.
All inputs are finite; a program needn't handle non-finite values.
Results may differ from the reference program's by a relative error of at most 0.0003.
Values sent between devices are 32-bit elements; how exact they have to be, the bound alone decides.
A program may use at most 64 MiB of HBM per device.

```python
import math
import jax
import jax.numpy as jnp
from jax import lax

FACE = 128
TRACERS = 256
SUBSTEPS = 2
LEV = 4
COLS = 512


def double_peaked(key, buffer_dimensions, upper_band_fraction, lower_band_minimum, lower_band_maximum, upper_band_minimum, upper_band_maximum):
    chooser_key, lower_key, upper_key = jax.random.split(key, 3)
    chooser = jax.random.uniform(chooser_key, buffer_dimensions, jnp.float32)
    lower = jax.random.uniform(lower_key, buffer_dimensions, jnp.float32, lower_band_minimum, lower_band_maximum)
    upper = jax.random.uniform(upper_key, buffer_dimensions, jnp.float32, upper_band_minimum, upper_band_maximum)
    return jnp.where(chooser < upper_band_fraction, upper, lower)


def wind_pair(key, reverse_share, magnitude_floor):
    level_shape = (LEV, COLS, FACE)
    magnitude_key, sign_key, flip_key = jax.random.split(key, 3)
    magnitudes = jax.random.uniform(magnitude_key, (2,) + level_shape, jnp.float32, magnitude_floor, 1.0)
    first_sign = jnp.where(jax.random.uniform(sign_key, level_shape, jnp.float32) < 0.5, 1.0, -1.0)
    second_sign = jnp.where(jax.random.uniform(flip_key, level_shape, jnp.float32) < reverse_share, -first_sign, first_sign)
    return jnp.stack([first_sign, second_sign]) * magnitudes


def log_between(key, buffer_dimensions, lowest, highest):
    spread = jax.random.uniform(key, buffer_dimensions, jnp.float32)
    return lowest * jnp.exp(spread * math.log(highest / lowest))


def draw_tracers(key, part):
    key = jax.random.fold_in(key, 3)
    buffer_dimensions = (TRACERS, LEV, COLS, FACE)
    return double_peaked(key, buffer_dimensions, 0.5, 0.2, 0.3, 3.5, 5.0)


def draw_air_mass(key, part):
    key = jax.random.fold_in(key, 5)
    buffer_dimensions = (LEV, COLS, FACE)
    return log_between(key, buffer_dimensions, 1.5, 3.0)


def draw_wind_x(key, part):
    key = jax.random.fold_in(key, 7)
    return wind_pair(key, 0.75, 0.6)


def draw_wind_y(key, part):
    key = jax.random.fold_in(key, 11)
    return wind_pair(key, 0.75, 0.6)


def draw_spacing_x(key, part):
    key = jax.random.fold_in(key, 13)
    buffer_dimensions = (COLS, FACE)
    return double_peaked(key, buffer_dimensions, 0.75, 0.5, 0.6, 0.85, 1.0)


def draw_spacing_y(key, part):
    key = jax.random.fold_in(key, 17)
    buffer_dimensions = (COLS, FACE)
    return double_peaked(key, buffer_dimensions, 0.75, 0.5, 0.6, 0.85, 1.0)


def draw_edge_mass_x(key, part):
    key = jax.random.fold_in(key, 19)
    buffer_dimensions = (LEV, COLS, FACE)
    return double_peaked(key, buffer_dimensions, 0.667, 0.3, 0.4, 0.85, 1.0)


def draw_edge_mass_y(key, part):
    key = jax.random.fold_in(key, 23)
    buffer_dimensions = (LEV, COLS, FACE)
    return double_peaked(key, buffer_dimensions, 0.667, 0.3, 0.4, 0.85, 1.0)


def setup_inputs(seed: int = 0) -> dict:
    arg_keys = jax.random.split(jax.random.key(seed), 9)
    return {
        "tracers": draw_tracers(jax.random.fold_in(arg_keys[8], 71), 0),
        "air_mass": draw_air_mass(jax.random.fold_in(arg_keys[8], 71), 0),
        "wind_x": draw_wind_x(jax.random.fold_in(arg_keys[8], 71), 0),
        "wind_y": draw_wind_y(jax.random.fold_in(arg_keys[8], 71), 0),
        "spacing_x": draw_spacing_x(jax.random.fold_in(arg_keys[8], 71), 0),
        "spacing_y": draw_spacing_y(jax.random.fold_in(arg_keys[8], 71), 0),
        "edge_mass_x": draw_edge_mass_x(jax.random.fold_in(arg_keys[8], 71), 0),
        "edge_mass_y": draw_edge_mass_y(jax.random.fold_in(arg_keys[8], 71), 0),
    }


max_courant = 0.15


def take_slice(values, offset, finish, dimension):
    return lax.slice_in_dim(values, offset, finish, axis=dimension)


def face_value(extended, courant, dimension):
    face_count = courant.shape[dimension]
    full_length = extended.shape[dimension]
    interface = (7.0 * (take_slice(extended, 1, full_length - 2, dimension) + take_slice(extended, 2, full_length - 1, dimension)) - (take_slice(extended, 0, full_length - 3, dimension) + take_slice(extended, 3, full_length, dimension))) / 12.0
    edge_west = take_slice(interface, 0, face_count, dimension)
    edge_centre = take_slice(interface, 1, face_count + 1, dimension)
    edge_east = take_slice(interface, 2, face_count + 2, dimension)
    donor_west = take_slice(extended, 2, face_count + 2, dimension)
    donor_east = take_slice(extended, 3, face_count + 3, dimension)
    slope_west = edge_centre - edge_west
    curve_west = 6.0 * donor_west - 3.0 * (edge_west + edge_centre)
    forward = edge_centre - 0.5 * courant * (slope_west - (1.0 - 2.0 * courant / 3.0) * curve_west)
    back_speed = -courant
    slope_east = edge_east - edge_centre
    curve_east = 6.0 * donor_east - 3.0 * (edge_centre + edge_east)
    backward = edge_centre + 0.5 * back_speed * (slope_east + (1.0 - 2.0 * back_speed / 3.0) * curve_east)
    return jnp.where(courant > 0.0, forward, backward)


def flux_sweep(mixing, column_mass, extended, courant, mass_flux, dimension):
    face_count = courant.shape[dimension - 1]
    cell_count = face_count - 1
    face_values = face_value(extended, courant[None], dimension)
    tracer_flux = mass_flux[None] * face_values
    new_mass = column_mass - (take_slice(mass_flux, 1, face_count, dimension - 1) - take_slice(mass_flux, 0, cell_count, dimension - 1))
    tracer_mass = mixing * column_mass[None] - (take_slice(tracer_flux, 1, face_count, dimension) - take_slice(tracer_flux, 0, cell_count, dimension))
    return tracer_mass / new_mass[None], new_mass


def pad_rows(mixing):
    first_row = mixing[..., :1]
    last_row = mixing[..., -1:]
    return jnp.concatenate([first_row, first_row, first_row, mixing, last_row, last_row, last_row], axis=-1)


def advance(extended, column_mass, courant_x, flux_x, courant_y, flux_y):
    width_cells = column_mass.shape[1]
    mixing = extended[:, :, 3:3 + width_cells]
    mixing, column_mass = flux_sweep(mixing, column_mass, extended, courant_x, flux_x, 2)
    closed = jnp.zeros_like(courant_y[:, :, :1])
    courant_faces = jnp.concatenate([courant_y, closed], axis=2)
    flux_faces = jnp.concatenate([flux_y, closed], axis=2)
    return flux_sweep(mixing, column_mass, pad_rows(mixing), courant_faces, flux_faces, 3)


def wind_fields(winds, spacing, edge_mass, weight):
    wind_speed = (1.0 - weight) * winds[0] + weight * winds[1]
    courant = max_courant * wind_speed * spacing[None]
    return courant, courant * edge_mass


def level_fields(winds_x, winds_y, mass_x, mass_y, spacing_x, spacing_y, substep):
    weight = (2.0 * substep + 1.0) / (2.0 * SUBSTEPS)
    courant_x, flux_x = wind_fields(winds_x, spacing_x, mass_x, weight)
    courant_y, flux_y = wind_fields(winds_y, spacing_y, mass_y, weight)
    row_index = lax.broadcasted_iota(jnp.int32, courant_y.shape, 2)
    courant_y = jnp.where(row_index > 0, courant_y, jnp.zeros_like(courant_y))
    flux_y = jnp.where(row_index > 0, flux_y, jnp.zeros_like(flux_y))
    return courant_x, flux_x, courant_y, flux_y


def reference(tracers, air_mass, wind_x, wind_y, spacing_x, spacing_y, edge_mass_x, edge_mass_y):
    fields = []
    for substep in range(SUBSTEPS):
        courant_x, flux_x, courant_y, flux_y = level_fields(wind_x, wind_y, edge_mass_x, edge_mass_y, spacing_x, spacing_y, substep)
        fields.append((jnp.concatenate([courant_x, courant_x[:, :1]], axis=1), jnp.concatenate([flux_x, flux_x[:, :1]], axis=1), courant_y, flux_y))

    def advect_one(single):
        mixing = single[None]
        column_mass = air_mass
        for courant_x, flux_x, courant_y, flux_y in fields:
            extended = jnp.concatenate([mixing[:, :, -3:], mixing, mixing[:, :, :3]], axis=2)
            mixing, column_mass = advance(extended, column_mass, courant_x, flux_x, courant_y, flux_y)
        return mixing[0]

    return lax.map(advect_one, tracers)
```

```python
import functools

import jax
import jax.numpy as jnp
from jax import lax
from jax.experimental import pallas as pl
from jax.experimental.pallas import tpu as pltpu
from jax.sharding import PartitionSpec as P

SUBSTEPS = 2
max_courant = 0.15
MESH = pl.DeviceIdType.MESH
CHUNK = 8
LAG = 3
AHEAD = 2
WIDTH = 8
HALO = 6


def face_weights(courant, flux):
    speed = jnp.abs(courant)
    half = 0.5 * speed
    bend = 3.0 * half * (1.0 - 2.0 * speed / 3.0)
    centre = flux * (1.0 - half - bend) / 12.0
    upwind = flux * (half - bend) / 12.0
    donor = 2.0 * flux * bend
    east = courant > 0.0
    zero = jnp.zeros_like(courant)
    up_p, up_n = jnp.where(east, upwind, zero), jnp.where(east, zero, upwind)
    don_p, don_n = jnp.where(east, donor, zero), jnp.where(east, zero, donor)
    return (
        -up_p,
        7.0 * up_p - centre,
        7.0 * (up_p + centre) - up_n + don_p,
        7.0 * (up_n + centre) - up_p + don_n,
        7.0 * up_n - centre,
        -up_n,
    )


def cell_weights(faces, shift, mass, new_mass):
    zero = jnp.zeros_like(mass)
    near = faces + (zero,)
    far = (zero,) + tuple(shift(w) for w in faces)
    inverse = 1.0 / new_mass
    out = []
    for j in range(7):
        total = near[j] - far[j]
        if j == 3:
            total = total + mass
        out.append(total * inverse)
    return out


def kernel(
    ring,
    tracers,
    air,
    wind_x,
    wind_y,
    space_x,
    space_y,
    edge_x,
    edge_y,
    out,
    q,
    res,
    fld,
    mine,
    raw,
    kw,
    load_sem,
    loc_sem,
    pin_s,
    pin_r,
    own_s,
    own_r,
    rel_s,
    rel_r,
    fin_sem,
    out_s,
    out_r,
    gat_s,
    gat_r,
    air_s,
    air_r,
    edge_s,
    edge_r,
):
    count = tracers.shape[0]
    chunks = count // CHUNK
    t = lax.axis_index("tracer")
    c = lax.axis_index("cols")
    core, hi = t % 2, t // 2
    par, s = c % 2, c // 2
    here = 2 * s
    group = (hi + par) % 2
    base = 2 * group
    away = 2 - base
    partner = (t, here + 1 - par)
    up = (t, 2 * ((s + 1) % ring) + par)
    down = (t, 2 * ((s + ring - 1) % ring) + par)
    other = 2 * hi + 1 - core
    across = 2 * (1 - hi) + core
    across_other = 2 * (1 - hi) + 1 - core

    barrier = pltpu.get_barrier_semaphore()
    peers = [
        partner,
        up,
        down,
        (other, here),
        (other, here + 1),
        (across, here),
        (across, here + 1),
        (across_other, here),
        (across_other, here + 1),
    ]
    peers[3] = (other, here + par)
    peers[4] = (other, here + 1 - par)
    for peer in peers:
        pl.semaphore_signal(barrier, inc=1, device_id=peer, device_id_type=MESH)

    loads = [
        pltpu.make_async_copy(wind_x.at[0, 0], raw.at[0], load_sem.at[0]),
        pltpu.make_async_copy(wind_x.at[1, 0], raw.at[1], load_sem.at[1]),
        pltpu.make_async_copy(wind_y.at[0, 0], raw.at[2], load_sem.at[2]),
        pltpu.make_async_copy(wind_y.at[1, 0], raw.at[3], load_sem.at[3]),
        pltpu.make_async_copy(space_x, raw.at[4], load_sem.at[4]),
        pltpu.make_async_copy(space_y, raw.at[5], load_sem.at[5]),
        pltpu.make_async_copy(edge_x.at[0], mine.at[4], load_sem.at[6]),
        pltpu.make_async_copy(edge_y.at[0], mine.at[5], load_sem.at[7]),
        pltpu.make_async_copy(
            air.at[pl.ds(base, 2)], fld.at[:, 6, pl.ds(pl.multiple_of(8 + 8 * par, 8), 8)], load_sem.at[8]
        ),
    ]
    for copy in loads:
        copy.start()

    def rows_of(k):
        return pl.ds(pl.multiple_of(k * CHUNK, CHUNK), CHUNK)

    def each_column(body):
        def step(i, carry):
            body(i // WIDTH, i % WIDTH)
            return carry

        lax.fori_loop(0, 2 * WIDTH, step, 0)

    def local_in(k):
        def one(l, col):
            pltpu.make_async_copy(
                tracers.at[rows_of(k), base + l, col],
                q.at[l, HALO + WIDTH * par + col, rows_of(k)],
                loc_sem.at[k],
            ).start()

        each_column(one)

    def tile_of(k, side):
        return q.at[:, pl.ds(HALO + WIDTH * side, WIDTH), rows_of(k)]

    def wait_local(k):
        pltpu.make_async_copy(tile_of(k, par), tile_of(k, par), loc_sem.at[k]).wait()

    def pair_in(k):
        def one(l, col):
            pltpu.make_async_remote_copy(
                src_ref=tracers.at[rows_of(k), away + l, col],
                dst_ref=q.at[l, HALO + WIDTH * par + col, rows_of(k)],
                send_sem=pin_s.at[k],
                recv_sem=pin_r.at[k],
                device_id=partner,
                device_id_type=MESH,
            ).start()

        each_column(one)

    def pair_in_all(k):
        return pltpu.make_async_remote_copy(
            src_ref=tile_of(k, par),
            dst_ref=tile_of(k, 1 - par),
            send_sem=pin_s.at[k],
            recv_sem=pin_r.at[k],
            device_id=partner,
            device_id_type=MESH,
        )

    def own_halo(k):
        return pltpu.make_async_remote_copy(
            src_ref=q.at[:, pl.ds(HALO + 10 * par, HALO), rows_of(k)],
            dst_ref=q.at[:, pl.ds((HALO + 2 * WIDTH) * (1 - par), HALO), rows_of(k)],
            send_sem=own_s.at[k],
            recv_sem=own_r.at[k],
            device_id=(t, 2 * ((s + ring - 1 + 2 * par) % ring) + par),
            device_id_type=MESH,
        )

    def relay_halo(k):
        return pltpu.make_async_remote_copy(
            src_ref=q.at[:, pl.ds(HALO + 10 * (1 - par), HALO), rows_of(k)],
            dst_ref=q.at[:, pl.ds((HALO + 2 * WIDTH) * par, HALO), rows_of(k)],
            send_sem=rel_s.at[k],
            recv_sem=rel_r.at[k],
            device_id=(t, 2 * ((s + ring + 1 - 2 * par) % ring) + par),
            device_id_type=MESH,
        )

    def send_out(k):
        def one(l, col):
            pltpu.make_async_remote_copy(
                src_ref=res.at[l, WIDTH * (1 - par) + col, rows_of(k)],
                dst_ref=out.at[rows_of(k), base + l, col],
                send_sem=out_s.at[k],
                recv_sem=out_r.at[k],
                device_id=partner,
                device_id_type=MESH,
            ).start()

        each_column(one)

    def out_all(k):
        side = res.at[:, pl.ds(WIDTH * (1 - par), WIDTH), rows_of(k)]
        return pltpu.make_async_remote_copy(
            src_ref=side,
            dst_ref=out.at[rows_of(k), pl.ds(away, 2)],
            send_sem=out_s.at[k],
            recv_sem=out_r.at[k],
            device_id=partner,
            device_id_type=MESH,
        )

    def keep_out(k):
        def one(l, col):
            pltpu.make_async_copy(
                res.at[l, WIDTH * par + col, rows_of(k)],
                out.at[rows_of(k), base + l, col],
                fin_sem.at[k],
            ).start()

        each_column(one)

    def wait_keep(k):
        part = out.at[rows_of(k), pl.ds(base, 2)]
        pltpu.make_async_copy(part, part, fin_sem.at[k]).wait()

    for k in range(chunks):
        local_in(k)

    pl.semaphore_wait(barrier, len(peers))
    for k in range(min(AHEAD, chunks)):
        pair_in(k)

    for copy in loads:
        copy.wait()
    for direction in range(2):
        for substep in range(SUBSTEPS):
            weight = (2.0 * substep + 1.0) / (2.0 * SUBSTEPS)
            wind = (1.0 - weight) * raw[2 * direction] + weight * raw[2 * direction + 1]
            courant = max_courant * wind * raw[4 + direction]
            if direction == 1:
                row = lax.broadcasted_iota(jnp.int32, courant.shape, 1)
                courant = jnp.where(row > 0, courant, jnp.zeros_like(courant))
            mine[2 * direction + substep] = courant

    place = fld.at[core, pl.ds(0, 6), pl.ds(pl.multiple_of(8 + 8 * par, 8), 8)]
    slot = 2 * core + par

    def gather_to(n, device):
        return pltpu.make_async_remote_copy(
            src_ref=mine,
            dst_ref=place,
            send_sem=gat_s.at[n],
            recv_sem=gat_r.at[slot],
            device_id=device,
            device_id_type=MESH,
        )

    gathers = [
        gather_to(1, (other, here)),
        gather_to(2, (across, here + 1)),
        gather_to(3, (across_other, here + 1)),
    ]
    to_partner = gather_to(0, partner)
    to_self = pltpu.make_async_copy(mine, place, gat_r.at[slot])

    @pl.when(par == 0)
    def _():
        to_self.start()
        gathers[0].start()

    @pl.when(par == 1)
    def _():
        to_partner.start()
        gathers[0].start()

    gathers[1].start()
    gathers[2].start()
    air_copy = pltpu.make_async_remote_copy(
        src_ref=air.at[pl.ds(away, 2)],
        dst_ref=fld.at[:, 6, pl.ds(pl.multiple_of(8 + 8 * par, 8), 8)],
        send_sem=air_s.at[0],
        recv_sem=air_r.at[0],
        device_id=partner,
        device_id_type=MESH,
    )
    air_copy.start()
    for k in range(chunks):
        wait_local(k)
        own_halo(k).start()

    for n in range(4):
        part = fld.at[n // 2, pl.ds(0, 6), pl.ds(8 + 8 * (n % 2), 8)]
        pltpu.make_async_copy(part, part, gat_r.at[n]).wait()
    air_copy.wait_recv()

    edge_down = pltpu.make_async_remote_copy(
        src_ref=fld.at[:, :, pl.ds(8, 4)],
        dst_ref=fld.at[:, :, pl.ds(24, 4)],
        send_sem=edge_s.at[0],
        recv_sem=edge_r.at[0],
        device_id=down,
        device_id_type=MESH,
    )
    edge_up = pltpu.make_async_remote_copy(
        src_ref=fld.at[:, :, pl.ds(21, 3)],
        dst_ref=fld.at[:, :, pl.ds(5, 3)],
        send_sem=edge_s.at[1],
        recv_sem=edge_r.at[1],
        device_id=up,
        device_id_type=MESH,
    )
    edge_down.start()
    edge_up.start()

    def weights():
        edge_down.wait_recv()
        edge_up.wait_recv()

        def level(l, carry):
            mass = fld[l, 6]
            shape = mass.shape
            row = lax.broadcasted_iota(jnp.int32, shape, 1)
            last = shape[1] - 1
            for sub in range(SUBSTEPS):
                courant_x, courant_y = fld[l, sub], fld[l, 2 + sub]
                flux_x, flux_y = courant_x * fld[l, 4], courant_y * fld[l, 5]

                def next_x(v):
                    return pltpu.roll(v, shape[0] - 1, axis=0)

                def next_y(v):
                    return pltpu.roll(v, shape[1] - 1, axis=1)

                new_mass = mass - (next_x(flux_x) - flux_x)
                kx = cell_weights(face_weights(courant_x, flux_x), next_x, mass, new_mass)
                mass = new_mass
                new_mass = mass - (next_y(flux_y) - flux_y)
                ky = cell_weights(face_weights(courant_y, flux_y), next_y, mass, new_mass)
                mass = new_mass
                for side in (-1, 1):
                    for reach in (3, 2):
                        far, near = 3 + side * reach, 3 + side * (reach - 1)
                        outside = (row < reach) if side < 0 else (row > last - reach)
                        moved = jnp.where(outside, ky[far], 0.0)
                        ky[near] = ky[near] + moved
                        ky[far] = ky[far] - moved
                    far = 3 + side
                    outside = (row < 1) if side < 0 else (row > last - 1)
                    moved = jnp.where(outside, ky[far], 0.0)
                    ky[3] = ky[3] + moved
                    ky[far] = ky[far] - moved
                for j in range(7):
                    kw[l, sub, j] = kx[j]
                kw[l, sub, 7] = ky[3]
                kw[l, sub, 8] = ky[2]
                kw[l, sub, 9] = pltpu.roll(ky[1], shape[1] - 2, axis=1)
                kw[l, sub, 10] = pltpu.roll(ky[0], shape[1] - 2, axis=1)
                kw[l, sub, 11] = pltpu.roll(ky[5], 2, axis=1)
                kw[l, sub, 12] = pltpu.roll(ky[4], 2, axis=1)
                kw[l, sub, 13] = ky[6]
            return carry

        lax.fori_loop(0, 2, level, 0)

    def sweep(l, sub, row, cells):
        def w(j):
            return kw[l, sub, j, pl.ds(row, 1), :]

        x = w(0) * cells[0]
        for j in range(1, 7):
            x = x + w(j) * cells[j]
        lanes = x.shape[1]
        before = pltpu.roll(x, 1, axis=1)
        total = w(7) * x + w(8) * before
        total = total + pltpu.roll(w(9) * x + w(10) * before, 2, axis=1)
        total = total + pltpu.roll(w(11) * x + w(12) * before, lanes - 2, axis=1)
        return total + w(13) * pltpu.roll(x, lanes - 3, axis=1)

    def compute(k):
        rows = rows_of(k)

        def level(l, carry):
            start = [q[l, i, rows, :] for i in range(2 * WIDTH + 2 * HALO)]
            middle = [sweep(l, 0, 5 + i, start[i : i + 7]) for i in range(2 * WIDTH + HALO)]
            for i in range(2 * WIDTH):
                res[l, i, rows, :] = sweep(l, 1, 8 + i, middle[i : i + 7])
            return carry

        lax.fori_loop(0, 2, level, 0)

    def step(k, carry):
        @pl.when(k < chunks)
        def _():
            pair_in_all(k).wait_recv()
            relay_halo(k).start()

        @pl.when(k + AHEAD < chunks)
        def _():
            pair_in(k + AHEAD)

        @pl.when(k == LAG)
        def _():
            weights()

        @pl.when(k >= LAG)
        def _():
            done = k - LAG
            own_halo(done).wait_recv()
            relay_halo(done).wait_recv()
            compute(done)
            send_out(done)
            keep_out(done)

        return carry

    lax.fori_loop(0, chunks + LAG, step, 0)

    def finish(k, carry):
        pair_in_all(k).wait_send()
        own_halo(k).wait_send()
        relay_halo(k).wait_send()
        wait_keep(k)
        out_all(k).wait_send()
        out_all(k).wait_recv()
        return carry

    lax.fori_loop(0, chunks, finish, 0)

    for gather in gathers:
        gather.wait_send()

    @pl.when(par == 1)
    def _():
        to_partner.wait_send()

    air_copy.wait_send()
    edge_down.wait_send()
    edge_up.wait_send()


def on_device(ring, tracers, *others):
    count, levels, columns, rows = tracers.shape
    chunks = count // CHUNK
    anywhere = pl.BlockSpec(memory_space=pl.ANY)
    dma = pltpu.SemaphoreType.DMA
    f32 = jnp.float32
    return pl.pallas_call(
        functools.partial(kernel, ring),
        out_shape=jax.ShapeDtypeStruct(tracers.shape, f32),
        in_specs=[anywhere] * 8,
        out_specs=anywhere,
        scratch_shapes=[
            pltpu.VMEM((2, 2 * WIDTH + 2 * HALO, count, rows), f32),
            pltpu.VMEM((2, 2 * WIDTH, count, rows), f32),
            pltpu.VMEM((2, 7, 4 * WIDTH, rows), f32),
            pltpu.VMEM((6, WIDTH, rows), f32),
            pltpu.VMEM((6, WIDTH, rows), f32),
            pltpu.VMEM((2, SUBSTEPS, 14, 4 * WIDTH, rows), f32),
            dma((9,)),
            dma((chunks,)),
            dma((chunks,)),
            dma((chunks,)),
            dma((chunks,)),
            dma((chunks,)),
            dma((chunks,)),
            dma((chunks,)),
            dma((chunks,)),
            dma((chunks,)),
            dma((chunks,)),
            dma((4,)),
            dma((4,)),
            dma((1,)),
            dma((1,)),
            dma((2,)),
            dma((2,)),
        ],
        compiler_params=pltpu.CompilerParams(
            collective_id=0, has_side_effects=True, vmem_limit_bytes=56 * 2**20
        ),
        cost_estimate=pl.CostEstimate(
            flops=2 * 13 * 4 * tracers.size, bytes_accessed=8 * tracers.size, transcendentals=0
        ),
        name="transport",
    )(tracers, *others)


def solution(mesh):
    placed = (
        P("tracer", None, "cols", None),
        P(None, "cols", None),
        P(None, "tracer", "cols", None),
        P(None, "tracer", "cols", None),
        P("cols", None),
        P("cols", None),
        P("tracer", "cols", None),
        P("tracer", "cols", None),
    )
    return jax.shard_map(
        functools.partial(on_device, mesh.shape["cols"] // 2),
        mesh=mesh,
        in_specs=placed,
        out_specs=P("tracer", None, "cols", None),
        check_vma=False,
    )
```

```python
import functools

import jax
import jax.numpy as jnp
from jax import lax
from jax.experimental import pallas as pl
from jax.experimental.pallas import tpu as pltpu
from jax.sharding import PartitionSpec as P

SUBSTEPS = 2
max_courant = 0.15
MESH = pl.DeviceIdType.MESH
CHUNK = 8
LAG = 4
AHEAD = 3
SPREAD = 0
EDGE = 1
WIDTH = 8
HALO = 6


def face_weights(courant, flux):
    speed = jnp.abs(courant)
    half = 0.5 * speed
    bend = 3.0 * half * (1.0 - 2.0 * speed / 3.0)
    centre = flux * (1.0 - half - bend) / 12.0
    upwind = flux * (half - bend) / 12.0
    donor = 2.0 * flux * bend
    east = courant > 0.0
    zero = jnp.zeros_like(courant)
    up_p, up_n = jnp.where(east, upwind, zero), jnp.where(east, zero, upwind)
    don_p, don_n = jnp.where(east, donor, zero), jnp.where(east, zero, donor)
    return (
        -up_p,
        7.0 * up_p - centre,
        7.0 * (up_p + centre) - up_n + don_p,
        7.0 * (up_n + centre) - up_p + don_n,
        7.0 * up_n - centre,
        -up_n,
    )


def cell_weights(faces, shift, mass, new_mass):
    zero = jnp.zeros_like(mass)
    near = faces + (zero,)
    far = (zero,) + tuple(shift(w) for w in faces)
    inverse = 1.0 / new_mass
    out = []
    for j in range(7):
        total = near[j] - far[j]
        if j == 3:
            total = total + mass
        out.append(total * inverse)
    return out


def kernel(
    ring,
    tracers,
    air,
    wind_x,
    wind_y,
    space_x,
    space_y,
    edge_x,
    edge_y,
    out,
    tile,
    halo,
    res,
    fld,
    mine,
    raw,
    kw,
    met,
    load_sem,
    loc_sem,
    pin_s,
    pin_r,
    own_s,
    own_r,
    rel_s,
    rel_r,
    fin_sem,
    out_s,
    out_r,
    one_s,
    one_r,
    two_s,
    two_r,
    air_s,
    air_r,
):
    count = tracers.shape[0]
    chunks = count // CHUNK
    t = lax.axis_index("tracer")
    c = lax.axis_index("cols")
    core, hi = t % 2, t // 2
    par, s = c % 2, c // 2
    here = 2 * s
    group = (hi + par) % 2
    base = 2 * group
    away = 2 - base
    partner = (t, here + 1 - par)
    up = (t, 2 * ((s + 1) % ring) + par)
    down = (t, 2 * ((s + ring - 1) % ring) + par)
    other = 2 * hi + 1 - core
    across = 2 * (1 - hi) + core
    across_other = 2 * (1 - hi) + 1 - core

    barrier = pltpu.get_barrier_semaphore()
    first = 2 * hi
    first_across = 2 * (1 - hi)
    sibling = (other, c)

    def enter(device):
        pl.semaphore_signal(barrier, inc=1, device_id=device, device_id_type=MESH)

    @pl.when(core == 1)
    def _():
        enter((first, here + par))

    enter((first, here + 1 - par))
    enter((first_across, here + par))
    enter((first_across, here + 1 - par))

    loads = [
        pltpu.make_async_copy(wind_x.at[0, 0], raw.at[0], load_sem.at[0]),
        pltpu.make_async_copy(wind_x.at[1, 0], raw.at[1], load_sem.at[1]),
        pltpu.make_async_copy(wind_y.at[0, 0], raw.at[2], load_sem.at[2]),
        pltpu.make_async_copy(wind_y.at[1, 0], raw.at[3], load_sem.at[3]),
        pltpu.make_async_copy(space_x, raw.at[4], load_sem.at[4]),
        pltpu.make_async_copy(space_y, raw.at[5], load_sem.at[5]),
        pltpu.make_async_copy(edge_x.at[0], mine.at[4], load_sem.at[6]),
        pltpu.make_async_copy(edge_y.at[0], mine.at[5], load_sem.at[7]),
        pltpu.make_async_copy(
            air.at[pl.ds(base, 2)], fld.at[:, 6, pl.ds(pl.multiple_of(8 + 8 * par, 8), 8)], load_sem.at[8]
        ),
    ]
    for copy in loads:
        copy.start()

    def rows_of(k):
        return pl.ds(pl.multiple_of(k * CHUNK, CHUNK), CHUNK)

    def remote(src, dst, send, recv, k, device):
        return pltpu.make_async_remote_copy(
            src_ref=src,
            dst_ref=dst,
            send_sem=send.at[k],
            recv_sem=recv.at[k],
            device_id=device,
            device_id_type=MESH,
        )

    def local_in(k):
        rows = rows_of(k)
        return pltpu.make_async_copy(tracers.at[rows, pl.ds(base, 2)], tile.at[par, rows], loc_sem.at[k])

    def pair_in(k):
        rows = rows_of(k)
        return remote(tracers.at[rows, pl.ds(away, 2)], tile.at[par, rows], pin_s, pin_r, k, partner)

    def own_halo(k):
        rows = rows_of(k)
        return remote(
            tile.at[par, rows, :, pl.ds(2 * par, HALO)],
            halo.at[1 - par, rows, :, pl.ds(0, HALO)],
            own_s,
            own_r,
            k,
            (t, 2 * ((s + ring - 1 + 2 * par) % ring) + par),
        )

    def relay_halo(k):
        rows = rows_of(k)
        return remote(
            tile.at[1 - par, rows, :, pl.ds(2 * (1 - par), HALO)],
            halo.at[par, rows, :, pl.ds(0, HALO)],
            rel_s,
            rel_r,
            k,
            (t, 2 * ((s + ring + 1 - 2 * par) % ring) + par),
        )

    def send_out(k):
        rows = rows_of(k)
        return remote(res.at[1 - par, rows], out.at[rows, pl.ds(base, 2)], out_s, out_r, k, partner)

    def keep_out(k):
        rows = rows_of(k)
        return pltpu.make_async_copy(res.at[par, rows], out.at[rows, pl.ds(base, 2)], fin_sem.at[k])

    for k in range(chunks):
        local_in(k).start()

    for copy in loads:
        copy.wait()
    for direction in range(2):
        for substep in range(SUBSTEPS):
            weight = (2.0 * substep + 1.0) / (2.0 * SUBSTEPS)
            wind = (1.0 - weight) * raw[2 * direction] + weight * raw[2 * direction + 1]
            courant = max_courant * wind * raw[4 + direction]
            if direction == 1:
                row = lax.broadcasted_iota(jnp.int32, courant.shape, 1)
                courant = jnp.where(row > 0, courant, jnp.zeros_like(courant))
            mine[2 * direction + substep] = courant

    @pl.when(par == 0)
    def _():
        fld[core, 0:6, WIDTH : 2 * WIDTH] = mine[...]

    @pl.when(core == 0)
    def _():
        pl.semaphore_wait(barrier, 7)
        pl.semaphore_signal(met, inc=1, device_id=sibling, device_id_type=MESH)
        enter((first + 1, up[1]))
        enter((first + 1, down[1]))

    @pl.when(core == 1)
    def _():
        pl.semaphore_wait(met, 1)

    whole = pl.ds(0, 6)
    west = pl.ds(WIDTH - 3, 3)
    east = pl.ds(3 * WIDTH, 4)
    parts = (pl.ds(WIDTH, WIDTH), pl.ds(2 * WIDTH, WIDTH), west, east)
    odd_tile = remote(mine, fld.at[core, whole, pl.ds(2 * WIDTH, WIDTH)], one_s, one_r, 0, partner)
    odd_edge = remote(mine.at[:, pl.ds(5, 3)], fld.at[core, whole, west], one_s, one_r, 1, (t, up[1] - par))
    even_edge = remote(mine.at[:, pl.ds(0, 4)], fld.at[core, whole, east], one_s, one_r, 2, (t, down[1] - par))
    spread = []
    for n, device in enumerate([(other, here), (across, here + 1), (across_other, here + 1)]):
        spread.append(
            [
                remote(
                    fld.at[core, whole, part],
                    fld.at[core, whole, part],
                    two_s.at[n],
                    two_r.at[core],
                    m,
                    device,
                )
                for m, part in enumerate(parts)
            ]
        )

    def spread_wait(slot):
        for m, part in enumerate(parts):
            place = fld.at[slot, whole, part]
            pltpu.make_async_copy(place, place, two_r.at[slot, m]).wait()

    air_pair = remote(
        air.at[pl.ds(away, 2)],
        fld.at[:, 6, pl.ds(pl.multiple_of(8 + 8 * par, 8), 8)],
        air_s.at[0],
        air_r,
        0,
        partner,
    )

    def air_edges(side, to):
        columns, place = ((pl.ds(0, 4), east), (pl.ds(5, 3), west))[side]
        return [
            remote(
                air.at[pl.ds(2 * ((hi + p) % 2), 2), columns],
                fld.at[:, 6, place],
                air_s.at[p + 1],
                air_r,
                2 - side,
                (t, to - side + p),
            )
            for p in range(2)
        ]

    @pl.when(par == 0)
    def _():
        for copies in spread:
            copies[0].start()

    @pl.when(par == 1)
    def _():
        odd_tile.start()

    air_pair.start()
    for k in range(min(AHEAD, chunks)):
        pair_in(k).start()

    @pl.when(core == 1)
    def _():
        pl.semaphore_wait(barrier, 2)
        pl.semaphore_signal(met, inc=1, device_id=sibling, device_id_type=MESH)

    @pl.when(core == 0)
    def _():
        pl.semaphore_wait(met, 1)

    @pl.when(par == 0)
    def _():
        even_edge.start()
        for copy in air_edges(0, down[1]):
            copy.start()

    @pl.when(par == 1)
    def _():
        odd_edge.start()
        for copy in air_edges(1, up[1]):
            copy.start()

    def fields_wait():
        air_pair.wait_recv()
        for side in range(2):
            place = fld.at[:, 6, (east, west)[side]]
            pltpu.make_async_copy(place, place, air_r.at[2 - side]).wait()

        @pl.when(par == 0)
        def _():
            spread_wait(1 - core)

        @pl.when(par == 1)
        def _():
            spread_wait(0)
            spread_wait(1)

    def weights():
        fields_wait()

        def level(l, carry):
            mass = fld[l, 6]
            shape = mass.shape
            row = lax.broadcasted_iota(jnp.int32, shape, 1)
            last = shape[1] - 1
            for sub in range(SUBSTEPS):
                courant_x, courant_y = fld[l, sub], fld[l, 2 + sub]
                flux_x, flux_y = courant_x * fld[l, 4], courant_y * fld[l, 5]

                def next_x(v):
                    return pltpu.roll(v, shape[0] - 1, axis=0)

                def next_y(v):
                    return pltpu.roll(v, shape[1] - 1, axis=1)

                new_mass = mass - (next_x(flux_x) - flux_x)
                kx = cell_weights(face_weights(courant_x, flux_x), next_x, mass, new_mass)
                mass = new_mass
                new_mass = mass - (next_y(flux_y) - flux_y)
                ky = cell_weights(face_weights(courant_y, flux_y), next_y, mass, new_mass)
                mass = new_mass
                for side in (-1, 1):
                    for reach in (3, 2):
                        far, near = 3 + side * reach, 3 + side * (reach - 1)
                        outside = (row < reach) if side < 0 else (row > last - reach)
                        moved = jnp.where(outside, ky[far], 0.0)
                        ky[near] = ky[near] + moved
                        ky[far] = ky[far] - moved
                    far = 3 + side
                    outside = (row < 1) if side < 0 else (row > last - 1)
                    moved = jnp.where(outside, ky[far], 0.0)
                    ky[3] = ky[3] + moved
                    ky[far] = ky[far] - moved
                for j in range(7):
                    kw[l, sub, j] = kx[j]
                kw[l, sub, 7] = ky[3]
                kw[l, sub, 8] = ky[2]
                kw[l, sub, 9] = pltpu.roll(ky[1], shape[1] - 2, axis=1)
                kw[l, sub, 10] = pltpu.roll(ky[0], shape[1] - 2, axis=1)
                kw[l, sub, 11] = pltpu.roll(ky[5], 2, axis=1)
                kw[l, sub, 12] = pltpu.roll(ky[4], 2, axis=1)
                kw[l, sub, 13] = ky[6]
            return carry

        lax.fori_loop(0, 2, level, 0)

    def sweep(l, sub, row, cells):
        def w(j):
            return kw[l, sub, j, pl.ds(row, 1), :]

        x = w(0) * cells[0]
        for j in range(1, 7):
            x = x + w(j) * cells[j]
        lanes = x.shape[1]
        before = pltpu.roll(x, 1, axis=1)
        total = w(7) * x + w(8) * before
        total = total + pltpu.roll(w(9) * x + w(10) * before, 2, axis=1)
        total = total + pltpu.roll(w(11) * x + w(12) * before, lanes - 2, axis=1)
        return total + w(13) * pltpu.roll(x, lanes - 3, axis=1)

    def flat(ref):
        return ref.reshape(2 * count * 2 * WIDTH, ref.shape[-1])

    def compute(k):
        def level(l, carry):
            def column(ref, side, col):
                row = ((side * count + k * CHUNK) * 2 + l) * WIDTH + col
                return flat(ref).at[pl.ds(row, CHUNK, stride=2 * WIDTH), :]

            start = [column(halo, 0, i)[...] for i in range(HALO)]
            start += [column(tile, side, i)[...] for side in range(2) for i in range(WIDTH)]
            start += [column(halo, 1, i)[...] for i in range(HALO)]
            middle = [sweep(l, 0, 5 + i, start[i : i + 7]) for i in range(2 * WIDTH + HALO)]
            for i in range(2 * WIDTH):
                column(res, i // WIDTH, i % WIDTH)[...] = sweep(l, 1, 8 + i, middle[i : i + 7])
            return carry

        lax.fori_loop(0, 2, level, 0)

    def step(k, carry):
        @pl.when(k < chunks)
        def _():
            pair_in(k).wait_recv()

            @pl.when(k + AHEAD < chunks)
            def _():
                pair_in(k + AHEAD).start()

            relay_halo(k).start()
            local_in(k).wait()
            own_halo(k).start()

        @pl.when((k == SPREAD) & (par == 0))
        def _():
            odd_tile.wait_recv()
            for copies in spread:
                copies[1].start()

        @pl.when((k == EDGE) & (par == 0))
        def _():
            odd_edge.wait_recv()
            even_edge.wait_recv()
            for copies in spread:
                copies[2].start()
                copies[3].start()

        @pl.when(k == LAG)
        def _():
            weights()

        @pl.when(k >= LAG)
        def _():
            done = k - LAG
            own_halo(done).wait_recv()
            relay_halo(done).wait_recv()
            compute(done)
            send_out(done).start()
            keep_out(done).start()

        return carry

    lax.fori_loop(0, chunks + LAG, step, 0)

    def finish(k, carry):
        pair_in(k).wait_send()
        own_halo(k).wait_send()
        relay_halo(k).wait_send()
        keep_out(k).wait()
        send_out(k).wait()
        return carry

    lax.fori_loop(0, chunks, finish, 0)

    air_pair.wait_send()

    @pl.when(par == 0)
    def _():
        even_edge.wait_send()
        for copy in air_edges(0, down[1]):
            copy.wait_send()
        for copies in spread:
            for copy in copies:
                copy.wait_send()

    @pl.when(par == 1)
    def _():
        odd_tile.wait_send()
        odd_edge.wait_send()
        for copy in air_edges(1, up[1]):
            copy.wait_send()


def on_device(ring, tracers, *others):
    count, levels, columns, rows = tracers.shape
    chunks = count // CHUNK
    anywhere = pl.BlockSpec(memory_space=pl.ANY)
    dma = pltpu.SemaphoreType.DMA
    f32 = jnp.float32
    return pl.pallas_call(
        functools.partial(kernel, ring),
        out_shape=pltpu.VMEM(tracers.shape, f32),
        in_specs=[anywhere] * 8,
        out_specs=pl.BlockSpec(memory_space=pltpu.VMEM),
        scratch_shapes=[
            pltpu.VMEM((2, count, 2, WIDTH, rows), f32),
            pltpu.VMEM((2, count, 2, WIDTH, rows), f32),
            pltpu.VMEM((2, count, 2, WIDTH, rows), f32),
            pltpu.VMEM((2, 7, 4 * WIDTH, rows), f32),
            pltpu.VMEM((6, WIDTH, rows), f32),
            pltpu.VMEM((6, WIDTH, rows), f32),
            pltpu.VMEM((2, SUBSTEPS, 14, 4 * WIDTH, rows), f32),
            pltpu.SemaphoreType.REGULAR,
            dma((9,)),
            dma((chunks,)),
            dma((chunks,)),
            dma((chunks,)),
            dma((chunks,)),
            dma((chunks,)),
            dma((chunks,)),
            dma((chunks,)),
            dma((chunks,)),
            dma((chunks,)),
            dma((chunks,)),
            dma((3,)),
            dma((3,)),
            dma((3, 4)),
            dma((2, 4)),
            dma((3, 3)),
            dma((3,)),
        ],
        compiler_params=pltpu.CompilerParams(
            collective_id=0, has_side_effects=True, vmem_limit_bytes=48 * 2**20
        ),
        cost_estimate=pl.CostEstimate(
            flops=2 * 13 * 4 * tracers.size, bytes_accessed=8 * tracers.size, transcendentals=0
        ),
        name="transport",
    )(*[pltpu.with_memory_space_constraint(a, pltpu.HBM) for a in (tracers, *others)])


def solution(mesh):
    placed = (
        P("tracer", None, "cols", None),
        P(None, "cols", None),
        P(None, "tracer", "cols", None),
        P(None, "tracer", "cols", None),
        P("cols", None),
        P("cols", None),
        P("tracer", "cols", None),
        P("tracer", "cols", None),
    )
    return jax.shard_map(
        functools.partial(on_device, mesh.shape["cols"] // 2),
        mesh=mesh,
        in_specs=placed,
        out_specs=P("tracer", None, "cols", None),
        check_vma=False,
    )
```

```python
import functools

import jax
import jax.numpy as jnp
from jax import lax
from jax.experimental import pallas as pl
from jax.experimental.pallas import tpu as pltpu
from jax.sharding import PartitionSpec as P

SUBSTEPS = 2
max_courant = 0.15
MESH = pl.DeviceIdType.MESH
CHUNK = 8
DIRECT = 2
LAG = 5
FIRST = 2
EARLY = 5
AHEAD = 3
SPREAD = 0
WIDTH = 8
HALO = 6


def face_weights(courant, flux):
    speed = jnp.abs(courant)
    half = 0.5 * speed
    bend = 3.0 * half * (1.0 - 2.0 * speed / 3.0)
    centre = flux * (1.0 - half - bend) / 12.0
    upwind = flux * (half - bend) / 12.0
    donor = 2.0 * flux * bend
    east = courant > 0.0
    zero = jnp.zeros_like(courant)
    up_p, up_n = jnp.where(east, upwind, zero), jnp.where(east, zero, upwind)
    don_p, don_n = jnp.where(east, donor, zero), jnp.where(east, zero, donor)
    return (
        -up_p,
        7.0 * up_p - centre,
        7.0 * (up_p + centre) - up_n + don_p,
        7.0 * (up_n + centre) - up_p + don_n,
        7.0 * up_n - centre,
        -up_n,
    )


def cell_weights(faces, shift, mass, new_mass):
    zero = jnp.zeros_like(mass)
    near = faces + (zero,)
    far = (zero,) + tuple(shift(w) for w in faces)
    inverse = 1.0 / new_mass
    out = []
    for j in range(7):
        total = near[j] - far[j]
        if j == 3:
            total = total + mass
        out.append(total * inverse)
    return out


def kernel(
    ring,
    tracers,
    air,
    wind_x,
    wind_y,
    space_x,
    space_y,
    edge_x,
    edge_y,
    out,
    tile,
    halo,
    res,
    fld,
    mine,
    raw,
    kw,
    met,
    load_sem,
    loc_sem,
    pin_s,
    pin_r,
    own_s,
    own_r,
    rel_s,
    rel_r,
    fin_sem,
    out_s,
    out_r,
    dir_s,
    one_s,
    one_r,
    two_s,
    two_r,
    edge_s,
    edge_r,
    air_s,
    air_r,
):
    count = tracers.shape[0]
    chunks = count // CHUNK
    t = lax.axis_index("tracer")
    c = lax.axis_index("cols")
    core, hi = t % 2, t // 2
    par, s = c % 2, c // 2
    here = 2 * s
    group = (hi + par + 1) % 2
    base = 2 * group
    away = 2 - base
    partner = (t, here + 1 - par)
    up = (t, 2 * ((s + 1) % ring) + par)
    down = (t, 2 * ((s + ring - 1) % ring) + par)
    other = 2 * hi + 1 - core
    across = 2 * (1 - hi) + core
    across_other = 2 * (1 - hi) + 1 - core

    barrier = pltpu.get_barrier_semaphore()

    def enter(device, column):
        pl.semaphore_signal(barrier, inc=1, device_id=(device, column), device_id_type=MESH)

    beside = (2 * ((s + 1) % ring) + 1, 2 * ((s + ring - 1) % ring) + 1)

    @pl.when(par == 1)
    def _():
        enter(*partner)
        enter(other, c)
        for column in beside:
            enter(t, column)
            enter(other, column)

    @pl.when(par == 0)
    def _():
        enter(across, here + 1)
        enter(across_other, here + 1)
        for column in beside:
            enter(t, column)
            enter(across, column)
            enter(across_other, column)

    loads = [
        pltpu.make_async_copy(wind_x.at[0, 0], raw.at[0], load_sem.at[0]),
        pltpu.make_async_copy(wind_x.at[1, 0], raw.at[1], load_sem.at[1]),
        pltpu.make_async_copy(wind_y.at[0, 0], raw.at[2], load_sem.at[2]),
        pltpu.make_async_copy(wind_y.at[1, 0], raw.at[3], load_sem.at[3]),
        pltpu.make_async_copy(space_x, raw.at[4], load_sem.at[4]),
        pltpu.make_async_copy(space_y, raw.at[5], load_sem.at[5]),
        pltpu.make_async_copy(edge_x.at[0], mine.at[4], load_sem.at[6]),
        pltpu.make_async_copy(edge_y.at[0], mine.at[5], load_sem.at[7]),
        pltpu.make_async_copy(
            air.at[pl.ds(base, 2)], fld.at[:, 6, pl.ds(pl.multiple_of(8 + 8 * par, 8), 8)], load_sem.at[8]
        ),
    ]
    for copy in loads:
        copy.start()

    def rows_of(k):
        return pl.ds(pl.multiple_of(k * CHUNK, CHUNK), CHUNK)

    def remote(src, dst, send, recv, k, device):
        return pltpu.make_async_remote_copy(
            src_ref=src,
            dst_ref=dst,
            send_sem=send.at[k],
            recv_sem=recv.at[k],
            device_id=device,
            device_id_type=MESH,
        )

    def local_in(k):
        rows = rows_of(k)
        return pltpu.make_async_copy(tracers.at[rows, pl.ds(base, 2)], tile.at[par, rows], loc_sem.at[k])

    def pair_in(k):
        rows = rows_of(k)
        return remote(tracers.at[rows, pl.ds(away, 2)], tile.at[par, rows], pin_s, pin_r, k, partner)

    def own_halo(k):
        rows = rows_of(k)
        return remote(
            tile.at[par, rows, :, pl.ds(2 * par, HALO)],
            halo.at[1 - par, rows, :, pl.ds(0, HALO)],
            own_s,
            own_r,
            k,
            (t, 2 * ((s + ring - 1 + 2 * par) % ring) + par),
        )

    def relay_halo(k):
        rows = rows_of(k)
        return remote(
            tile.at[1 - par, rows, :, pl.ds(2 * (1 - par), HALO)],
            halo.at[par, rows, :, pl.ds(0, HALO)],
            rel_s,
            rel_r,
            k,
            (t, 2 * ((s + ring + 1 - 2 * par) % ring) + par),
        )

    def direct_halo(k):
        rows = rows_of(k)
        return remote(
            tracers.at[rows, pl.ds(away, 2), pl.ds(2 * par, HALO)],
            halo.at[1 - par, rows, :, pl.ds(0, HALO)],
            dir_s,
            rel_r,
            k,
            (t, 2 * ((s + ring - 1 + 2 * par) % ring) + 1 - par),
        )

    own_to_first = (s + ring - 1 + 2 * par) % ring == 0
    relay_to_first = (s + ring + 1 - 2 * par) % ring == 0

    def relayed(k):
        return jnp.logical_not(relay_to_first & (k >= chunks - DIRECT))

    def send_out(k):
        rows = rows_of(k)
        return remote(res.at[1 - par, rows], out.at[rows, pl.ds(base, 2)], out_s, out_r, k, partner)

    def keep_out(k):
        rows = rows_of(k)
        return pltpu.make_async_copy(res.at[par, rows], out.at[rows, pl.ds(base, 2)], fin_sem.at[k])

    @pl.when(par == 0)
    def _():
        pl.semaphore_wait(barrier, 1)
        pl.semaphore_signal(met, inc=1, device_id=partner, device_id_type=MESH)

    @pl.when(par == 1)
    def _():
        pl.semaphore_wait(met, 1)

    for k in range(min(FIRST, chunks)):
        pair_in(k).start()
    for k in range(chunks):
        local_in(k).start()

    for copy in loads:
        copy.wait()
    for direction in range(2):
        for substep in range(SUBSTEPS):
            weight = (2.0 * substep + 1.0) / (2.0 * SUBSTEPS)
            wind = (1.0 - weight) * raw[2 * direction] + weight * raw[2 * direction + 1]
            courant = max_courant * wind * raw[4 + direction]
            if direction == 1:
                row = lax.broadcasted_iota(jnp.int32, courant.shape, 1)
                courant = jnp.where(row > 0, courant, jnp.zeros_like(courant))
            mine[2 * direction + substep] = courant

    @pl.when(par == 1)
    def _():
        fld[core, 0:6, 2 * WIDTH : 3 * WIDTH] = mine[...]

    whole = pl.ds(0, 6)
    west = pl.ds(WIDTH - 3, 3)
    east = pl.ds(3 * WIDTH, 4)
    tiles = (pl.ds(WIDTH, WIDTH), pl.ds(2 * WIDTH, WIDTH))
    even_tile = remote(mine, fld.at[core, whole, tiles[0]], one_s, one_r, 0, partner)
    sweepers = ((t, 1), (other, 1), (across, 0), (across_other, 0))

    def spread(m):
        place = fld.at[core, whole, tiles[m]]
        return [
            remote(place, place, two_s.at[n], two_r.at[core], m, (device, here + p))
            for n, (device, p) in enumerate(sweepers)
            if n > 0
        ]

    def spread_edge(m):
        start, place, column = ((WIDTH, east, down[1]), (3 * WIDTH - 3, west, up[1]))[m]
        return [
            remote(
                fld.at[core, whole, pl.ds(start, place.size)],
                fld.at[core, whole, place],
                edge_s.at[n],
                edge_r.at[core],
                m,
                (device, column - par + p),
            )
            for n, (device, p) in enumerate(sweepers)
        ]

    def spread_wait(slot):
        for m, part in enumerate(tiles):
            place = fld.at[slot, whole, part]
            pltpu.make_async_copy(place, place, two_r.at[slot, m]).wait()

    air_pair = remote(
        air.at[pl.ds(away, 2)],
        fld.at[:, 6, pl.ds(pl.multiple_of(8 + 8 * par, 8), 8)],
        air_s.at[0],
        air_r,
        0,
        partner,
    )

    def air_edges(side, to):
        columns, place = ((pl.ds(0, 4), east), (pl.ds(5, 3), west))[side]
        return [
            remote(
                air.at[pl.ds(2 * ((hi + p + 1) % 2), 2), columns],
                fld.at[:, 6, place],
                air_s.at[p + 1],
                air_r,
                2 - side,
                (t, to - side + p),
            )
            for p in range(2)
        ]

    @pl.when(par == 0)
    def _():
        even_tile.start()

    air_pair.start()
    for k in range(FIRST, min(AHEAD, chunks)):
        pair_in(k).start()

    @pl.when(s == 0)
    def _():
        for k in range(AHEAD, EARLY):
            pair_in(k).start()

    @pl.when(par == 1)
    def _():
        pl.semaphore_wait(barrier, 13)
        pl.semaphore_signal(met, inc=1, device_id=partner, device_id_type=MESH)
        for copy in spread(1) + spread_edge(1):
            copy.start()

    @pl.when(par == 0)
    def _():
        pl.semaphore_wait(met, 1)

    @pl.when(par == 0)
    def _():
        for copy in air_edges(0, down[1]):
            copy.start()

    @pl.when(par == 1)
    def _():
        for copy in air_edges(1, up[1]):
            copy.start()

    @pl.when(own_to_first)
    def _():
        for k in range(chunks - DIRECT, chunks):
            direct_halo(k).start()

    def fields_wait():
        air_pair.wait_recv()
        for slot in range(2):
            for m, part in enumerate((east, west)):
                place = fld.at[slot, whole, part]
                pltpu.make_async_copy(place, place, edge_r.at[slot, m]).wait()
        for side in range(2):
            place = fld.at[:, 6, (east, west)[side]]
            pltpu.make_async_copy(place, place, air_r.at[2 - side]).wait()

        @pl.when(par == 1)
        def _():
            spread_wait(1 - core)

        @pl.when(par == 0)
        def _():
            spread_wait(0)
            spread_wait(1)

    def weights():
        fields_wait()

        def level(l, carry):
            mass = fld[l, 6]
            shape = mass.shape
            row = lax.broadcasted_iota(jnp.int32, shape, 1)
            last = shape[1] - 1
            for sub in range(SUBSTEPS):
                courant_x, courant_y = fld[l, sub], fld[l, 2 + sub]
                flux_x, flux_y = courant_x * fld[l, 4], courant_y * fld[l, 5]

                def next_x(v):
                    return pltpu.roll(v, shape[0] - 1, axis=0)

                def next_y(v):
                    return pltpu.roll(v, shape[1] - 1, axis=1)

                new_mass = mass - (next_x(flux_x) - flux_x)
                kx = cell_weights(face_weights(courant_x, flux_x), next_x, mass, new_mass)
                mass = new_mass
                new_mass = mass - (next_y(flux_y) - flux_y)
                ky = cell_weights(face_weights(courant_y, flux_y), next_y, mass, new_mass)
                mass = new_mass
                for side in (-1, 1):
                    for reach in (3, 2):
                        far, near = 3 + side * reach, 3 + side * (reach - 1)
                        outside = (row < reach) if side < 0 else (row > last - reach)
                        moved = jnp.where(outside, ky[far], 0.0)
                        ky[near] = ky[near] + moved
                        ky[far] = ky[far] - moved
                    far = 3 + side
                    outside = (row < 1) if side < 0 else (row > last - 1)
                    moved = jnp.where(outside, ky[far], 0.0)
                    ky[3] = ky[3] + moved
                    ky[far] = ky[far] - moved
                for j in range(7):
                    kw[l, sub, j] = kx[j]
                kw[l, sub, 7] = ky[3]
                kw[l, sub, 8] = ky[2]
                kw[l, sub, 9] = pltpu.roll(ky[1], shape[1] - 2, axis=1)
                kw[l, sub, 10] = pltpu.roll(ky[0], shape[1] - 2, axis=1)
                kw[l, sub, 11] = pltpu.roll(ky[5], 2, axis=1)
                kw[l, sub, 12] = pltpu.roll(ky[4], 2, axis=1)
                kw[l, sub, 13] = ky[6]
            return carry

        lax.fori_loop(0, 2, level, 0)

    def sweep(l, sub, row, cells):
        def w(j):
            return kw[l, sub, j, pl.ds(row, 1), :]

        x = w(0) * cells[0]
        for j in range(1, 7):
            x = x + w(j) * cells[j]
        lanes = x.shape[1]
        before = pltpu.roll(x, 1, axis=1)
        total = w(7) * x + w(8) * before
        total = total + pltpu.roll(w(9) * x + w(10) * before, 2, axis=1)
        total = total + pltpu.roll(w(11) * x + w(12) * before, lanes - 2, axis=1)
        return total + w(13) * pltpu.roll(x, lanes - 3, axis=1)

    def flat(ref):
        return ref.reshape(2 * count * 2 * WIDTH, ref.shape[-1])

    def compute(k):
        def level(l, carry):
            def column(ref, side, col):
                row = ((side * count + k * CHUNK) * 2 + l) * WIDTH + col
                return flat(ref).at[pl.ds(row, CHUNK, stride=2 * WIDTH), :]

            start = [column(halo, 0, i)[...] for i in range(HALO)]
            start += [column(tile, side, i)[...] for side in range(2) for i in range(WIDTH)]
            start += [column(halo, 1, i)[...] for i in range(HALO)]
            middle = [sweep(l, 0, 5 + i, start[i : i + 7]) for i in range(2 * WIDTH + HALO)]
            for i in range(2 * WIDTH):
                column(res, i // WIDTH, i % WIDTH)[...] = sweep(l, 1, 8 + i, middle[i : i + 7])
            return carry

        lax.fori_loop(0, 2, level, 0)

    ahead = jnp.where(s > 0, AHEAD, EARLY)

    def step(k, carry):
        @pl.when(k < chunks)
        def _():
            pair_in(k).wait_recv()

            @pl.when(k + ahead < chunks)
            def _():
                pair_in(k + ahead).start()

            @pl.when(relayed(k))
            def _():
                relay_halo(k).start()


        @pl.when(2 * k < chunks)
        def _():
            for n in range(2):
                local_in(2 * k + n).wait()
                own_halo(2 * k + n).start()

        @pl.when((k == SPREAD) & (par == 1))
        def _():
            even_tile.wait_recv()
            for copy in spread_edge(0) + spread(0):
                copy.start()

        @pl.when(k == LAG)
        def _():
            weights()

        @pl.when(k >= LAG)
        def _():
            done = k - LAG
            own_halo(done).wait_recv()
            relay_halo(done).wait_recv()
            compute(done)
            send_out(done).start()
            keep_out(done).start()

        return carry

    lax.fori_loop(0, chunks + LAG, step, 0)

    def finish(k, carry):
        pair_in(k).wait_send()
        own_halo(k).wait_send()

        @pl.when(relayed(k))
        def _():
            relay_halo(k).wait_send()

        @pl.when(own_to_first & (k >= chunks - DIRECT))
        def _():
            direct_halo(k).wait_send()

        keep_out(k).wait()
        send_out(k).wait()
        return carry

    lax.fori_loop(0, chunks, finish, 0)

    air_pair.wait_send()

    @pl.when(par == 0)
    def _():
        even_tile.wait_send()
        for copy in air_edges(0, down[1]):
            copy.wait_send()

    @pl.when(par == 1)
    def _():
        for copy in spread(0) + spread(1) + spread_edge(0) + spread_edge(1) + air_edges(1, up[1]):
            copy.wait_send()


def on_device(ring, tracers, *others):
    count, levels, columns, rows = tracers.shape
    chunks = count // CHUNK
    anywhere = pl.BlockSpec(memory_space=pl.ANY)
    dma = pltpu.SemaphoreType.DMA
    f32 = jnp.float32
    return pl.pallas_call(
        functools.partial(kernel, ring),
        out_shape=pltpu.VMEM(tracers.shape, f32),
        in_specs=[anywhere] * 8,
        out_specs=pl.BlockSpec(memory_space=pltpu.VMEM),
        scratch_shapes=[
            pltpu.VMEM((2, count, 2, WIDTH, rows), f32),
            pltpu.VMEM((2, count, 2, WIDTH, rows), f32),
            pltpu.VMEM((2, count, 2, WIDTH, rows), f32),
            pltpu.VMEM((2, 7, 4 * WIDTH, rows), f32),
            pltpu.VMEM((6, WIDTH, rows), f32),
            pltpu.VMEM((6, WIDTH, rows), f32),
            pltpu.VMEM((2, SUBSTEPS, 14, 4 * WIDTH, rows), f32),
            pltpu.SemaphoreType.REGULAR,
            dma((9,)),
            dma((chunks,)),
            dma((chunks,)),
            dma((chunks,)),
            dma((chunks,)),
            dma((chunks,)),
            dma((chunks,)),
            dma((chunks,)),
            dma((chunks,)),
            dma((chunks,)),
            dma((chunks,)),
            dma((chunks,)),
            dma((1,)),
            dma((1,)),
            dma((4, 2)),
            dma((2, 2)),
            dma((4, 2)),
            dma((2, 2)),
            dma((3, 3)),
            dma((3,)),
        ],
        compiler_params=pltpu.CompilerParams(
            collective_id=0, has_side_effects=True, vmem_limit_bytes=48 * 2**20
        ),
        cost_estimate=pl.CostEstimate(
            flops=2 * 13 * 4 * tracers.size, bytes_accessed=8 * tracers.size, transcendentals=0
        ),
        name="transport",
    )(*[pltpu.with_memory_space_constraint(a, pltpu.HBM) for a in (tracers, *others)])


def solution(mesh):
    placed = (
        P("tracer", None, "cols", None),
        P(None, "cols", None),
        P(None, "tracer", "cols", None),
        P(None, "tracer", "cols", None),
        P("cols", None),
        P("cols", None),
        P("tracer", "cols", None),
        P("tracer", "cols", None),
    )
    return jax.shard_map(
        functools.partial(on_device, mesh.shape["cols"] // 2),
        mesh=mesh,
        in_specs=placed,
        out_specs=P("tracer", None, "cols", None),
        check_vma=False,
    )
```

```python
import functools

import jax
import jax.numpy as jnp
from jax import lax
from jax.experimental import pallas as pl
from jax.experimental.pallas import tpu as pltpu
from jax.sharding import PartitionSpec as P

SUBSTEPS = 2
max_courant = 0.15
MESH = pl.DeviceIdType.MESH
CHUNK = 8
LAG = 5
FIRST = 2
EARLY = 5
NAHEAD = 5
NLAG = 8
AHEAD = 3
SPREAD = 0
WIDTH = 8
HALO = 6


def face_weights(courant, flux):
    speed = jnp.abs(courant)
    half = 0.5 * speed
    bend = 3.0 * half * (1.0 - 2.0 * speed / 3.0)
    centre = flux * (1.0 - half - bend) / 12.0
    upwind = flux * (half - bend) / 12.0
    donor = 2.0 * flux * bend
    east = courant > 0.0
    zero = jnp.zeros_like(courant)
    up_p, up_n = jnp.where(east, upwind, zero), jnp.where(east, zero, upwind)
    don_p, don_n = jnp.where(east, donor, zero), jnp.where(east, zero, donor)
    return (
        -up_p,
        7.0 * up_p - centre,
        7.0 * (up_p + centre) - up_n + don_p,
        7.0 * (up_n + centre) - up_p + don_n,
        7.0 * up_n - centre,
        -up_n,
    )


def cell_weights(faces, shift, mass, new_mass):
    zero = jnp.zeros_like(mass)
    near = faces + (zero,)
    far = (zero,) + tuple(shift(w) for w in faces)
    inverse = 1.0 / new_mass
    out = []
    for j in range(7):
        total = near[j] - far[j]
        if j == 3:
            total = total + mass
        out.append(total * inverse)
    return out


def kernel(
    ring,
    tracers,
    air,
    wind_x,
    wind_y,
    space_x,
    space_y,
    edge_x,
    edge_y,
    out,
    tile,
    halo,
    res,
    fld,
    mine,
    raw,
    kw,
    met,
    load_sem,
    loc_sem,
    pin_s,
    pin_r,
    own_s,
    own_r,
    rel_s,
    rel_r,
    fin_sem,
    out_s,
    out_r,
    rest_s,
    rest_r,
    one_s,
    one_r,
    two_s,
    two_r,
    edge_s,
    edge_r,
    air_s,
    air_r,
):
    count = tracers.shape[0]
    chunks = count // CHUNK
    t = lax.axis_index("tracer")
    c = lax.axis_index("cols")
    core, hi = t % 2, t // 2
    par, s = c % 2, c // 2
    here = 2 * s
    group = (hi + par + 1) % 2
    base = 2 * group
    away = 2 - base
    partner = (t, here + 1 - par)
    up = (t, 2 * ((s + 1) % ring) + par)
    down = (t, 2 * ((s + ring - 1) % ring) + par)
    other = 2 * hi + 1 - core
    across = 2 * (1 - hi) + core
    across_other = 2 * (1 - hi) + 1 - core

    barrier = pltpu.get_barrier_semaphore()

    def enter(device, column):
        pl.semaphore_signal(barrier, inc=1, device_id=(device, column), device_id_type=MESH)

    beside = (2 * ((s + 1) % ring) + 1, 2 * ((s + ring - 1) % ring) + 1)

    @pl.when(par == 1)
    def _():
        enter(*partner)
        enter(other, c)
        for column in beside:
            enter(t, column)
            enter(other, column)

    @pl.when(par == 0)
    def _():
        enter(across, here + 1)
        enter(across_other, here + 1)
        for column in beside:
            enter(t, column)
            enter(across, column)
            enter(across_other, column)

    loads = [
        pltpu.make_async_copy(wind_x.at[0, 0], raw.at[0], load_sem.at[0]),
        pltpu.make_async_copy(wind_x.at[1, 0], raw.at[1], load_sem.at[1]),
        pltpu.make_async_copy(wind_y.at[0, 0], raw.at[2], load_sem.at[2]),
        pltpu.make_async_copy(wind_y.at[1, 0], raw.at[3], load_sem.at[3]),
        pltpu.make_async_copy(space_x, raw.at[4], load_sem.at[4]),
        pltpu.make_async_copy(space_y, raw.at[5], load_sem.at[5]),
        pltpu.make_async_copy(edge_x.at[0], mine.at[4], load_sem.at[6]),
        pltpu.make_async_copy(edge_y.at[0], mine.at[5], load_sem.at[7]),
        pltpu.make_async_copy(
            air.at[pl.ds(base, 2)], fld.at[:, 6, pl.ds(pl.multiple_of(8 + 8 * par, 8), 8)], load_sem.at[8]
        ),
    ]
    for copy in loads:
        copy.start()

    def rows_of(k):
        return pl.ds(pl.multiple_of(k * CHUNK, CHUNK), CHUNK)

    def remote(src, dst, send, recv, k, device):
        return pltpu.make_async_remote_copy(
            src_ref=src,
            dst_ref=dst,
            send_sem=send.at[k],
            recv_sem=recv.at[k],
            device_id=device,
            device_id_type=MESH,
        )

    def local_in(k):
        rows = rows_of(k)
        return pltpu.make_async_copy(tracers.at[rows, pl.ds(base, 2)], tile.at[par, rows], loc_sem.at[k])

    def pair_in(k):
        rows = rows_of(k)
        return remote(tracers.at[rows, pl.ds(away, 2)], tile.at[par, rows], pin_s, pin_r, k, partner)

    own_to_first = (s + ring - 1 + 2 * par) % ring == 0
    relay_to_first = (s + ring + 1 - 2 * par) % ring == 0

    def pair_part(k, start, columns, send, recv):
        rows, part = rows_of(k), pl.ds(start, columns)
        return remote(
            tracers.at[rows, pl.ds(away, 2), part], tile.at[par, rows, :, part], send, recv, k, partner
        )

    def pair_edge(k):
        return pair_part(k, 2 * par, HALO, pin_s, pin_r)

    def pair_rest(k):
        return pair_part(k, HALO * (1 - par), 2, rest_s, rest_r)

    def pair_start(k):
        @pl.when(own_to_first)
        def _():
            pair_edge(k).start()

        @pl.when(jnp.logical_not(own_to_first))
        def _():
            pair_in(k).start()

    def own_halo(k):
        rows = rows_of(k)
        return remote(
            tile.at[par, rows, :, pl.ds(2 * par, HALO)],
            halo.at[1 - par, rows, :, pl.ds(0, HALO)],
            own_s,
            own_r,
            k,
            (t, 2 * ((s + ring - 1 + 2 * par) % ring) + par),
        )

    def relay_halo(k):
        rows = rows_of(k)
        return remote(
            tile.at[1 - par, rows, :, pl.ds(2 * (1 - par), HALO)],
            halo.at[par, rows, :, pl.ds(0, HALO)],
            rel_s,
            rel_r,
            k,
            (t, 2 * ((s + ring + 1 - 2 * par) % ring) + par),
        )

    def send_out(k, l):
        rows = rows_of(k)
        return remote(res.at[1 - par, rows, l], out.at[rows, base + l], out_s, out_r, 2 * k + l, partner)

    def keep_out(k):
        rows = rows_of(k)
        return pltpu.make_async_copy(res.at[par, rows], out.at[rows, pl.ds(base, 2)], fin_sem.at[k])

    @pl.when(par == 0)
    def _():
        pl.semaphore_wait(barrier, 1)
        pl.semaphore_signal(met, inc=1, device_id=partner, device_id_type=MESH)

    @pl.when(par == 1)
    def _():
        pl.semaphore_wait(met, 1)

    for k in range(min(FIRST, chunks)):
        pair_start(k)
    for k in range(chunks):
        local_in(k).start()

    for copy in loads:
        copy.wait()
    for direction in range(2):
        for substep in range(SUBSTEPS):
            weight = (2.0 * substep + 1.0) / (2.0 * SUBSTEPS)
            wind = (1.0 - weight) * raw[2 * direction] + weight * raw[2 * direction + 1]
            courant = max_courant * wind * raw[4 + direction]
            if direction == 1:
                row = lax.broadcasted_iota(jnp.int32, courant.shape, 1)
                courant = jnp.where(row > 0, courant, jnp.zeros_like(courant))
            mine[2 * direction + substep] = courant

    @pl.when(par == 1)
    def _():
        fld[core, 0:6, 2 * WIDTH : 3 * WIDTH] = mine[...]

    whole = pl.ds(0, 6)
    west = pl.ds(WIDTH - 3, 3)
    east = pl.ds(3 * WIDTH, 4)
    tiles = (pl.ds(WIDTH, WIDTH), pl.ds(2 * WIDTH, WIDTH))
    even_tile = remote(mine, fld.at[core, whole, tiles[0]], one_s, one_r, 0, partner)
    sweepers = ((t, 1), (other, 1), (across, 0), (across_other, 0))

    def spread(m):
        place = fld.at[core, whole, tiles[m]]
        return [
            remote(place, place, two_s.at[n], two_r.at[core], m, (device, here + p))
            for n, (device, p) in enumerate(sweepers)
            if n > 0
        ]

    def spread_edge(m):
        start, place, column = ((WIDTH, east, down[1]), (3 * WIDTH - 3, west, up[1]))[m]
        return [
            remote(
                fld.at[core, whole, pl.ds(start, place.size)],
                fld.at[core, whole, place],
                edge_s.at[n],
                edge_r.at[core],
                m,
                (device, column - par + p),
            )
            for n, (device, p) in enumerate(sweepers)
        ]

    def spread_wait(slot):
        for m, part in enumerate(tiles):
            place = fld.at[slot, whole, part]
            pltpu.make_async_copy(place, place, two_r.at[slot, m]).wait()

    air_pair = remote(
        air.at[pl.ds(away, 2)],
        fld.at[:, 6, pl.ds(pl.multiple_of(8 + 8 * par, 8), 8)],
        air_s.at[0],
        air_r,
        0,
        partner,
    )

    def air_edges(side, to):
        columns, place = ((pl.ds(0, 4), east), (pl.ds(5, 3), west))[side]
        return [
            remote(
                air.at[pl.ds(2 * ((hi + p + 1) % 2), 2), columns],
                fld.at[:, 6, place],
                air_s.at[p + 1],
                air_r,
                2 - side,
                (t, to - side + p),
            )
            for p in range(2)
        ]

    @pl.when(par == 0)
    def _():
        even_tile.start()

    air_pair.start()
    for k in range(FIRST, min(AHEAD, chunks)):
        pair_start(k)

    @pl.when((s == 1) | (s == ring - 1))
    def _():
        for k in range(AHEAD, NAHEAD):
            pair_start(k)

    @pl.when(s == 0)
    def _():
        for k in range(AHEAD, EARLY):
            pair_start(k)

    @pl.when(par == 1)
    def _():
        pl.semaphore_wait(barrier, 13)
        pl.semaphore_signal(met, inc=1, device_id=partner, device_id_type=MESH)
        for copy in spread(1) + spread_edge(1):
            copy.start()

    @pl.when(par == 0)
    def _():
        pl.semaphore_wait(met, 1)

    @pl.when(par == 0)
    def _():
        for copy in air_edges(0, down[1]):
            copy.start()

    @pl.when(par == 1)
    def _():
        for copy in air_edges(1, up[1]):
            copy.start()

    def fields_wait():
        air_pair.wait_recv()
        for slot in range(2):
            for m, part in enumerate((east, west)):
                place = fld.at[slot, whole, part]
                pltpu.make_async_copy(place, place, edge_r.at[slot, m]).wait()
        for side in range(2):
            place = fld.at[:, 6, (east, west)[side]]
            pltpu.make_async_copy(place, place, air_r.at[2 - side]).wait()

        @pl.when(par == 1)
        def _():
            spread_wait(1 - core)

        @pl.when(par == 0)
        def _():
            spread_wait(0)
            spread_wait(1)

    def weights():
        fields_wait()

        def level(l, carry):
            mass = fld[l, 6]
            shape = mass.shape
            row = lax.broadcasted_iota(jnp.int32, shape, 1)
            last = shape[1] - 1
            for sub in range(SUBSTEPS):
                courant_x, courant_y = fld[l, sub], fld[l, 2 + sub]
                flux_x, flux_y = courant_x * fld[l, 4], courant_y * fld[l, 5]

                def next_x(v):
                    return pltpu.roll(v, shape[0] - 1, axis=0)

                def next_y(v):
                    return pltpu.roll(v, shape[1] - 1, axis=1)

                new_mass = mass - (next_x(flux_x) - flux_x)
                kx = cell_weights(face_weights(courant_x, flux_x), next_x, mass, new_mass)
                mass = new_mass
                new_mass = mass - (next_y(flux_y) - flux_y)
                ky = cell_weights(face_weights(courant_y, flux_y), next_y, mass, new_mass)
                mass = new_mass
                for side in (-1, 1):
                    for reach in (3, 2):
                        far, near = 3 + side * reach, 3 + side * (reach - 1)
                        outside = (row < reach) if side < 0 else (row > last - reach)
                        moved = jnp.where(outside, ky[far], 0.0)
                        ky[near] = ky[near] + moved
                        ky[far] = ky[far] - moved
                    far = 3 + side
                    outside = (row < 1) if side < 0 else (row > last - 1)
                    moved = jnp.where(outside, ky[far], 0.0)
                    ky[3] = ky[3] + moved
                    ky[far] = ky[far] - moved
                for j in range(7):
                    kw[l, sub, j] = kx[j]
                kw[l, sub, 7] = ky[3]
                kw[l, sub, 8] = ky[2]
                kw[l, sub, 9] = pltpu.roll(ky[1], shape[1] - 2, axis=1)
                kw[l, sub, 10] = pltpu.roll(ky[0], shape[1] - 2, axis=1)
                kw[l, sub, 11] = pltpu.roll(ky[5], 2, axis=1)
                kw[l, sub, 12] = pltpu.roll(ky[4], 2, axis=1)
                kw[l, sub, 13] = ky[6]
            return carry

        lax.fori_loop(0, 2, level, 0)

    def sweep(l, sub, row, cells):
        def w(j):
            return kw[l, sub, j, pl.ds(row, 1), :]

        x = w(0) * cells[0]
        for j in range(1, 7):
            x = x + w(j) * cells[j]
        lanes = x.shape[1]
        before = pltpu.roll(x, 1, axis=1)
        total = w(7) * x + w(8) * before
        total = total + pltpu.roll(w(9) * x + w(10) * before, 2, axis=1)
        total = total + pltpu.roll(w(11) * x + w(12) * before, lanes - 2, axis=1)
        return total + w(13) * pltpu.roll(x, lanes - 3, axis=1)

    def flat(ref):
        return ref.reshape(2 * count * 2 * WIDTH, ref.shape[-1])

    def compute(k):
        def level(l, carry):
            def column(ref, side, col):
                row = ((side * count + k * CHUNK) * 2 + l) * WIDTH + col
                return flat(ref).at[pl.ds(row, CHUNK, stride=2 * WIDTH), :]

            start = [column(halo, 0, i)[...] for i in range(HALO)]
            start += [column(tile, side, i)[...] for side in range(2) for i in range(WIDTH)]
            start += [column(halo, 1, i)[...] for i in range(HALO)]
            middle = [sweep(l, 0, 5 + i, start[i : i + 7]) for i in range(2 * WIDTH + HALO)]
            for i in range(2 * WIDTH):
                column(res, i // WIDTH, i % WIDTH)[...] = sweep(l, 1, 8 + i, middle[i : i + 7])
            send_out(k, l).start()
            return carry

        lax.fori_loop(0, 2, level, 0)

    next_first = (s == 1) | (s == ring - 1)
    ahead = jnp.where(s > 0, jnp.where(next_first, NAHEAD, AHEAD), EARLY)
    lag = jnp.where(next_first, NLAG, LAG)

    def step(k, carry):
        @pl.when(k < chunks)
        def _():
            @pl.when(relay_to_first)
            def _():
                pair_edge(k).wait_recv()

            @pl.when(jnp.logical_not(relay_to_first))
            def _():
                pair_in(k).wait_recv()

            @pl.when(k + ahead < chunks)
            def _():
                pair_start(k + ahead)

            relay_halo(k).start()


        rest = 2 * (k - (chunks - NAHEAD))

        @pl.when(own_to_first & (rest >= 0) & (rest < chunks))
        def _():
            for n in range(2):
                pair_rest(rest + n).start()

        @pl.when(2 * k < chunks)
        def _():
            for n in range(2):
                local_in(2 * k + n).wait()
                own_halo(2 * k + n).start()

        @pl.when((k == SPREAD) & (par == 1))
        def _():
            even_tile.wait_recv()
            for copy in spread_edge(0) + spread(0):
                copy.start()

        @pl.when(k == lag)
        def _():
            weights()

        @pl.when((k >= lag) & (k < chunks + lag))
        def _():
            done = k - lag

            @pl.when(relay_to_first)
            def _():
                pair_rest(done).wait_recv()

            own_halo(done).wait_recv()
            relay_halo(done).wait_recv()
            compute(done)
            keep_out(done).start()

        return carry

    lax.fori_loop(0, chunks + max(LAG, NLAG), step, 0)

    def finish(k, carry):
        @pl.when(own_to_first)
        def _():
            pair_edge(k).wait_send()
            pair_rest(k).wait_send()

        @pl.when(jnp.logical_not(own_to_first))
        def _():
            pair_in(k).wait_send()

        own_halo(k).wait_send()

        relay_halo(k).wait_send()
        keep_out(k).wait()
        for l in range(2):
            send_out(k, l).wait()
        return carry

    lax.fori_loop(0, chunks, finish, 0)

    air_pair.wait_send()

    @pl.when(par == 0)
    def _():
        even_tile.wait_send()
        for copy in air_edges(0, down[1]):
            copy.wait_send()

    @pl.when(par == 1)
    def _():
        for copy in spread(0) + spread(1) + spread_edge(0) + spread_edge(1) + air_edges(1, up[1]):
            copy.wait_send()


def on_device(ring, tracers, *others):
    count, levels, columns, rows = tracers.shape
    chunks = count // CHUNK
    anywhere = pl.BlockSpec(memory_space=pl.ANY)
    dma = pltpu.SemaphoreType.DMA
    f32 = jnp.float32
    return pl.pallas_call(
        functools.partial(kernel, ring),
        out_shape=pltpu.VMEM(tracers.shape, f32),
        in_specs=[anywhere] * 8,
        out_specs=pl.BlockSpec(memory_space=pltpu.VMEM),
        scratch_shapes=[
            pltpu.VMEM((2, count, 2, WIDTH, rows), f32),
            pltpu.VMEM((2, count, 2, WIDTH, rows), f32),
            pltpu.VMEM((2, count, 2, WIDTH, rows), f32),
            pltpu.VMEM((2, 7, 4 * WIDTH, rows), f32),
            pltpu.VMEM((6, WIDTH, rows), f32),
            pltpu.VMEM((6, WIDTH, rows), f32),
            pltpu.VMEM((2, SUBSTEPS, 14, 4 * WIDTH, rows), f32),
            pltpu.SemaphoreType.REGULAR,
            dma((9,)),
            dma((chunks,)),
            dma((chunks,)),
            dma((chunks,)),
            dma((chunks,)),
            dma((chunks,)),
            dma((chunks,)),
            dma((chunks,)),
            dma((chunks,)),
            dma((2 * chunks,)),
            dma((2 * chunks,)),
            dma((chunks,)),
            dma((chunks,)),
            dma((1,)),
            dma((1,)),
            dma((4, 2)),
            dma((2, 2)),
            dma((4, 2)),
            dma((2, 2)),
            dma((3, 3)),
            dma((3,)),
        ],
        compiler_params=pltpu.CompilerParams(
            collective_id=0, has_side_effects=True, vmem_limit_bytes=48 * 2**20
        ),
        cost_estimate=pl.CostEstimate(
            flops=2 * 13 * 4 * tracers.size, bytes_accessed=8 * tracers.size, transcendentals=0
        ),
        name="transport",
    )(*[pltpu.with_memory_space_constraint(a, pltpu.HBM) for a in (tracers, *others)])


def solution(mesh):
    placed = (
        P("tracer", None, "cols", None),
        P(None, "cols", None),
        P(None, "tracer", "cols", None),
        P(None, "tracer", "cols", None),
        P("cols", None),
        P("cols", None),
        P("tracer", "cols", None),
        P("tracer", "cols", None),
    )
    return jax.shard_map(
        functools.partial(on_device, mesh.shape["cols"] // 2),
        mesh=mesh,
        in_specs=placed,
        out_specs=P("tracer", None, "cols", None),
        check_vma=False,
    )
```

```python
import functools

import jax
import jax.numpy as jnp
from jax import lax
from jax.experimental import pallas as pl
from jax.experimental.pallas import tpu as pltpu
from jax.sharding import PartitionSpec as P

SUBSTEPS = 2
max_courant = 0.15
MESH = pl.DeviceIdType.MESH
CHUNK = 8
LAG = 5
FIRST = 2
EARLY = 5
NAHEAD = 5
RESTS = 8
NLAG = 8
AHEAD = 3
SPREAD = 0
WIDTH = 8
HALO = 6


def face_weights(courant, flux):
    speed = jnp.abs(courant)
    half = 0.5 * speed
    bend = 3.0 * half * (1.0 - 2.0 * speed / 3.0)
    centre = flux * (1.0 - half - bend) / 12.0
    upwind = flux * (half - bend) / 12.0
    donor = 2.0 * flux * bend
    east = courant > 0.0
    zero = jnp.zeros_like(courant)
    up_p, up_n = jnp.where(east, upwind, zero), jnp.where(east, zero, upwind)
    don_p, don_n = jnp.where(east, donor, zero), jnp.where(east, zero, donor)
    return (
        -up_p,
        7.0 * up_p - centre,
        7.0 * (up_p + centre) - up_n + don_p,
        7.0 * (up_n + centre) - up_p + don_n,
        7.0 * up_n - centre,
        -up_n,
    )


def cell_weights(faces, shift, mass, new_mass):
    zero = jnp.zeros_like(mass)
    near = faces + (zero,)
    far = (zero,) + tuple(shift(w) for w in faces)
    inverse = 1.0 / new_mass
    out = []
    for j in range(7):
        total = near[j] - far[j]
        if j == 3:
            total = total + mass
        out.append(total * inverse)
    return out


def kernel(
    ring,
    tracers,
    air,
    wind_x,
    wind_y,
    space_x,
    space_y,
    edge_x,
    edge_y,
    out,
    tile,
    halo,
    res,
    fld,
    mine,
    raw,
    kw,
    met,
    load_sem,
    loc_sem,
    pin_s,
    pin_r,
    own_s,
    own_r,
    rel_s,
    rel_r,
    fin_sem,
    out_s,
    out_r,
    rest_s,
    rest_r,
    one_s,
    one_r,
    two_s,
    two_r,
    edge_s,
    edge_r,
    air_s,
    air_r,
):
    count = tracers.shape[0]
    chunks = count // CHUNK
    t = lax.axis_index("tracer")
    c = lax.axis_index("cols")
    core, hi = t % 2, t // 2
    par, s = c % 2, c // 2
    here = 2 * s
    group = (hi + par + 1) % 2
    base = 2 * group
    away = 2 - base
    partner = (t, here + 1 - par)
    up = (t, 2 * ((s + 1) % ring) + par)
    down = (t, 2 * ((s + ring - 1) % ring) + par)
    other = 2 * hi + 1 - core
    across = 2 * (1 - hi) + core
    across_other = 2 * (1 - hi) + 1 - core

    barrier = pltpu.get_barrier_semaphore()

    def enter(device, column):
        pl.semaphore_signal(barrier, inc=1, device_id=(device, column), device_id_type=MESH)

    beside = (2 * ((s + 1) % ring) + 1, 2 * ((s + ring - 1) % ring) + 1)

    @pl.when(par == 1)
    def _():
        enter(*partner)
        enter(other, c)
        for column in beside:
            enter(t, column)
            enter(other, column)

    @pl.when(par == 0)
    def _():
        enter(across, here + 1)
        enter(across_other, here + 1)
        for column in beside:
            enter(t, column)
            enter(across, column)
            enter(across_other, column)

    loads = [
        pltpu.make_async_copy(wind_x.at[0, 0], raw.at[0], load_sem.at[0]),
        pltpu.make_async_copy(wind_x.at[1, 0], raw.at[1], load_sem.at[1]),
        pltpu.make_async_copy(wind_y.at[0, 0], raw.at[2], load_sem.at[2]),
        pltpu.make_async_copy(wind_y.at[1, 0], raw.at[3], load_sem.at[3]),
        pltpu.make_async_copy(space_x, raw.at[4], load_sem.at[4]),
        pltpu.make_async_copy(space_y, raw.at[5], load_sem.at[5]),
        pltpu.make_async_copy(edge_x.at[0], mine.at[4], load_sem.at[6]),
        pltpu.make_async_copy(edge_y.at[0], mine.at[5], load_sem.at[7]),
        pltpu.make_async_copy(
            air.at[pl.ds(base, 2)], fld.at[:, 6, pl.ds(pl.multiple_of(8 + 8 * par, 8), 8)], load_sem.at[8]
        ),
    ]
    for copy in loads:
        copy.start()

    def rows_of(k):
        return pl.ds(pl.multiple_of(k * CHUNK, CHUNK), CHUNK)

    def remote(src, dst, send, recv, k, device):
        return pltpu.make_async_remote_copy(
            src_ref=src,
            dst_ref=dst,
            send_sem=send.at[k],
            recv_sem=recv.at[k],
            device_id=device,
            device_id_type=MESH,
        )

    def local_in(k):
        rows = rows_of(k)
        return pltpu.make_async_copy(tracers.at[rows, pl.ds(base, 2)], tile.at[par, rows], loc_sem.at[k])

    def pair_in(k):
        rows = rows_of(k)
        return remote(tracers.at[rows, pl.ds(away, 2)], tile.at[par, rows], pin_s, pin_r, k, partner)

    own_to_first = (s + ring - 1 + 2 * par) % ring == 0
    relay_to_first = (s + ring + 1 - 2 * par) % ring == 0

    def pair_part(k, rows, start, columns, send, recv):
        part = pl.ds(start, columns)
        return remote(
            tracers.at[rows, pl.ds(away, 2), part], tile.at[par, rows, :, part], send, recv, k, partner
        )

    def pair_edge(k):
        return pair_part(k, rows_of(k), 2 * par, HALO, pin_s, pin_r)

    def pair_rest(n):
        rows = pl.ds(pl.multiple_of(n * RESTS * CHUNK, CHUNK), RESTS * CHUNK)
        return pair_part(n, rows, HALO * (1 - par), 2, rest_s, rest_r)

    def pair_start(k):
        @pl.when(own_to_first)
        def _():
            pair_edge(k).start()

        @pl.when(jnp.logical_not(own_to_first))
        def _():
            pair_in(k).start()

    def own_halo(k):
        rows = rows_of(k)
        return remote(
            tile.at[par, rows, :, pl.ds(2 * par, HALO)],
            halo.at[1 - par, rows, :, pl.ds(0, HALO)],
            own_s,
            own_r,
            k,
            (t, 2 * ((s + ring - 1 + 2 * par) % ring) + par),
        )

    def relay_halo(k):
        rows = rows_of(k)
        return remote(
            tile.at[1 - par, rows, :, pl.ds(2 * (1 - par), HALO)],
            halo.at[par, rows, :, pl.ds(0, HALO)],
            rel_s,
            rel_r,
            k,
            (t, 2 * ((s + ring + 1 - 2 * par) % ring) + par),
        )

    def send_out(k, l):
        rows = rows_of(k)
        return remote(res.at[1 - par, rows, l], out.at[rows, base + l], out_s, out_r, 2 * k + l, partner)

    def keep_out(k):
        rows = rows_of(k)
        return pltpu.make_async_copy(res.at[par, rows], out.at[rows, pl.ds(base, 2)], fin_sem.at[k])

    @pl.when(par == 0)
    def _():
        pl.semaphore_wait(barrier, 1)
        pl.semaphore_signal(met, inc=1, device_id=partner, device_id_type=MESH)

    @pl.when(par == 1)
    def _():
        pl.semaphore_wait(met, 1)

    for k in range(min(FIRST, chunks)):
        pair_start(k)
    for k in range(chunks):
        local_in(k).start()

    for copy in loads:
        copy.wait()
    for direction in range(2):
        for substep in range(SUBSTEPS):
            weight = (2.0 * substep + 1.0) / (2.0 * SUBSTEPS)
            wind = (1.0 - weight) * raw[2 * direction] + weight * raw[2 * direction + 1]
            courant = max_courant * wind * raw[4 + direction]
            if direction == 1:
                row = lax.broadcasted_iota(jnp.int32, courant.shape, 1)
                courant = jnp.where(row > 0, courant, jnp.zeros_like(courant))
            mine[2 * direction + substep] = courant

    @pl.when(par == 1)
    def _():
        fld[core, 0:6, 2 * WIDTH : 3 * WIDTH] = mine[...]

    whole = pl.ds(0, 6)
    west = pl.ds(WIDTH - 3, 3)
    east = pl.ds(3 * WIDTH, 4)
    tiles = (pl.ds(WIDTH, WIDTH), pl.ds(2 * WIDTH, WIDTH))
    even_tile = remote(mine, fld.at[core, whole, tiles[0]], one_s, one_r, 0, partner)
    sweepers = ((t, 1), (other, 1), (across, 0), (across_other, 0))

    def spread(m):
        place = fld.at[core, whole, tiles[m]]
        return [
            remote(place, place, two_s.at[n], two_r.at[core], m, (device, here + p))
            for n, (device, p) in enumerate(sweepers)
            if n > 0
        ]

    def spread_edge(m):
        start, place, column = ((WIDTH, east, down[1]), (3 * WIDTH - 3, west, up[1]))[m]
        return [
            remote(
                fld.at[core, whole, pl.ds(start, place.size)],
                fld.at[core, whole, place],
                edge_s.at[n],
                edge_r.at[core],
                m,
                (device, column - par + p),
            )
            for n, (device, p) in enumerate(sweepers)
        ]

    def spread_wait(slot):
        for m, part in enumerate(tiles):
            place = fld.at[slot, whole, part]
            pltpu.make_async_copy(place, place, two_r.at[slot, m]).wait()

    air_pair = remote(
        air.at[pl.ds(away, 2)],
        fld.at[:, 6, pl.ds(pl.multiple_of(8 + 8 * par, 8), 8)],
        air_s.at[0],
        air_r,
        0,
        partner,
    )

    def air_edges(side, to):
        columns, place = ((pl.ds(0, 4), east), (pl.ds(5, 3), west))[side]
        return [
            remote(
                air.at[pl.ds(2 * ((hi + p + 1) % 2), 2), columns],
                fld.at[:, 6, place],
                air_s.at[p + 1],
                air_r,
                2 - side,
                (t, to - side + p),
            )
            for p in range(2)
        ]

    @pl.when(par == 0)
    def _():
        even_tile.start()

    air_pair.start()
    for k in range(FIRST, min(AHEAD, chunks)):
        pair_start(k)

    @pl.when((s == 1) | (s == ring - 1))
    def _():
        for k in range(AHEAD, NAHEAD):
            pair_start(k)

    @pl.when(s == 0)
    def _():
        for k in range(AHEAD, EARLY):
            pair_start(k)

    @pl.when(par == 1)
    def _():
        pl.semaphore_wait(barrier, 13)
        pl.semaphore_signal(met, inc=1, device_id=partner, device_id_type=MESH)
        for copy in spread(1) + spread_edge(1):
            copy.start()

    @pl.when(par == 0)
    def _():
        pl.semaphore_wait(met, 1)

    @pl.when(par == 0)
    def _():
        for copy in air_edges(0, down[1]):
            copy.start()

    @pl.when(par == 1)
    def _():
        for copy in air_edges(1, up[1]):
            copy.start()

    def fields_wait():
        air_pair.wait_recv()
        for slot in range(2):
            for m, part in enumerate((east, west)):
                place = fld.at[slot, whole, part]
                pltpu.make_async_copy(place, place, edge_r.at[slot, m]).wait()
        for side in range(2):
            place = fld.at[:, 6, (east, west)[side]]
            pltpu.make_async_copy(place, place, air_r.at[2 - side]).wait()

        @pl.when(par == 1)
        def _():
            spread_wait(1 - core)

        @pl.when(par == 0)
        def _():
            spread_wait(0)
            spread_wait(1)

    def weights():
        fields_wait()

        def level(l, carry):
            mass = fld[l, 6]
            shape = mass.shape
            row = lax.broadcasted_iota(jnp.int32, shape, 1)
            last = shape[1] - 1
            for sub in range(SUBSTEPS):
                courant_x, courant_y = fld[l, sub], fld[l, 2 + sub]
                flux_x, flux_y = courant_x * fld[l, 4], courant_y * fld[l, 5]

                def next_x(v):
                    return pltpu.roll(v, shape[0] - 1, axis=0)

                def next_y(v):
                    return pltpu.roll(v, shape[1] - 1, axis=1)

                new_mass = mass - (next_x(flux_x) - flux_x)
                kx = cell_weights(face_weights(courant_x, flux_x), next_x, mass, new_mass)
                mass = new_mass
                new_mass = mass - (next_y(flux_y) - flux_y)
                ky = cell_weights(face_weights(courant_y, flux_y), next_y, mass, new_mass)
                mass = new_mass
                for side in (-1, 1):
                    for reach in (3, 2):
                        far, near = 3 + side * reach, 3 + side * (reach - 1)
                        outside = (row < reach) if side < 0 else (row > last - reach)
                        moved = jnp.where(outside, ky[far], 0.0)
                        ky[near] = ky[near] + moved
                        ky[far] = ky[far] - moved
                    far = 3 + side
                    outside = (row < 1) if side < 0 else (row > last - 1)
                    moved = jnp.where(outside, ky[far], 0.0)
                    ky[3] = ky[3] + moved
                    ky[far] = ky[far] - moved
                for j in range(7):
                    kw[l, sub, j] = kx[j]
                kw[l, sub, 7] = ky[3]
                kw[l, sub, 8] = ky[2]
                kw[l, sub, 9] = pltpu.roll(ky[1], shape[1] - 2, axis=1)
                kw[l, sub, 10] = pltpu.roll(ky[0], shape[1] - 2, axis=1)
                kw[l, sub, 11] = pltpu.roll(ky[5], 2, axis=1)
                kw[l, sub, 12] = pltpu.roll(ky[4], 2, axis=1)
                kw[l, sub, 13] = ky[6]
            return carry

        lax.fori_loop(0, 2, level, 0)

    def sweep(l, sub, row, cells):
        def w(j):
            return kw[l, sub, j, pl.ds(row, 1), :]

        x = w(0) * cells[0]
        for j in range(1, 7):
            x = x + w(j) * cells[j]
        lanes = x.shape[1]
        before = pltpu.roll(x, 1, axis=1)
        total = w(7) * x + w(8) * before
        total = total + pltpu.roll(w(9) * x + w(10) * before, 2, axis=1)
        total = total + pltpu.roll(w(11) * x + w(12) * before, lanes - 2, axis=1)
        return total + w(13) * pltpu.roll(x, lanes - 3, axis=1)

    def flat(ref):
        return ref.reshape(3 * count * 2 * WIDTH, ref.shape[-1])

    def compute(k):
        def level(l, carry):
            def column(ref, side, col):
                row = ((side * count + k * CHUNK) * 2 + l) * WIDTH + col
                return flat(ref).at[pl.ds(row, CHUNK, stride=2 * WIDTH), :]

            start = [column(halo, 0, i)[...] for i in range(HALO)]
            start += [column(tile, side, i)[...] for side in range(2) for i in range(WIDTH)]
            start += [column(halo, 1, i)[...] for i in range(HALO)]
            middle = [sweep(l, 0, 5 + i, start[i : i + 7]) for i in range(2 * WIDTH + HALO)]
            for i in range(2 * WIDTH):
                column(res, i // WIDTH, i % WIDTH)[...] = sweep(l, 1, 8 + i, middle[i : i + 7])
            send_out(k, l).start()
            return carry

        lax.fori_loop(0, 2, level, 0)

    next_first = (s == 1) | (s == ring - 1)
    ahead = jnp.where(s > 0, jnp.where(next_first, NAHEAD, AHEAD), EARLY)
    lag = jnp.where(next_first, NLAG, LAG)

    def step(k, carry):
        @pl.when(k < chunks)
        def _():
            @pl.when(relay_to_first)
            def _():
                pair_edge(k).wait_recv()

            @pl.when(jnp.logical_not(relay_to_first))
            def _():
                pair_in(k).wait_recv()

            @pl.when(k + ahead < chunks)
            def _():
                pair_start(k + ahead)

            relay_halo(k).start()


        rest = k - (chunks - NAHEAD)

        @pl.when(own_to_first & (rest >= 0) & (rest < chunks // RESTS))
        def _():
            pair_rest(rest).start()

        @pl.when(2 * k < chunks)
        def _():
            for n in range(2):
                local_in(2 * k + n).wait()
                own_halo(2 * k + n).start()

        @pl.when((k == SPREAD) & (par == 1))
        def _():
            even_tile.wait_recv()
            for copy in spread_edge(0) + spread(0):
                copy.start()

        @pl.when(k == lag)
        def _():
            weights()

        @pl.when((k >= lag) & (k < chunks + lag))
        def _():
            done = k - lag

            @pl.when(relay_to_first & (done % RESTS == 0))
            def _():
                pair_rest(done // RESTS).wait_recv()

            own_halo(done).wait_recv()
            relay_halo(done).wait_recv()
            compute(done)
            keep_out(done).start()

        return carry

    lax.fori_loop(0, chunks + max(LAG, NLAG), step, 0)

    air_pair.wait_send()

    @pl.when(par == 0)
    def _():
        even_tile.wait_send()
        for copy in air_edges(0, down[1]):
            copy.wait_send()

    @pl.when(par == 1)
    def _():
        for copy in spread(0) + spread(1) + spread_edge(0) + spread_edge(1) + air_edges(1, up[1]):
            copy.wait_send()

    def sent(k, carry):
        @pl.when(own_to_first)
        def _():
            pair_edge(k).wait_send()

        @pl.when(jnp.logical_not(own_to_first))
        def _():
            pair_in(k).wait_send()

        own_halo(k).wait_send()
        relay_halo(k).wait_send()
        return carry

    lax.fori_loop(0, chunks, sent, 0)

    @pl.when(own_to_first)
    def _():
        for n in range(chunks // RESTS):
            pair_rest(n).wait_send()

    def finish(k, carry):
        keep_out(k).wait()
        for l in range(2):
            send_out(k, l).wait()
        return carry

    lax.fori_loop(0, chunks, finish, 0)


def on_device(ring, tracers, *others):
    count, levels, columns, rows = tracers.shape
    chunks = count // CHUNK
    anywhere = pl.BlockSpec(memory_space=pl.ANY)
    dma = pltpu.SemaphoreType.DMA
    f32 = jnp.float32
    return pl.pallas_call(
        functools.partial(kernel, ring),
        out_shape=pltpu.VMEM(tracers.shape, f32),
        in_specs=[anywhere] * 8,
        out_specs=pl.BlockSpec(memory_space=pltpu.VMEM),
        scratch_shapes=[
            pltpu.VMEM((3, count, 2, WIDTH, rows), f32),
            pltpu.VMEM((3, count, 2, WIDTH, rows), f32),
            pltpu.VMEM((3, count, 2, WIDTH, rows), f32),
            pltpu.VMEM((2, 7, 4 * WIDTH, rows), f32),
            pltpu.VMEM((6, WIDTH, rows), f32),
            pltpu.VMEM((6, WIDTH, rows), f32),
            pltpu.VMEM((2, SUBSTEPS, 14, 4 * WIDTH, rows), f32),
            pltpu.SemaphoreType.REGULAR,
            dma((9,)),
            dma((chunks,)),
            dma((chunks,)),
            dma((chunks,)),
            dma((chunks,)),
            dma((chunks,)),
            dma((chunks,)),
            dma((chunks,)),
            dma((chunks,)),
            dma((2 * chunks,)),
            dma((2 * chunks,)),
            dma((chunks,)),
            dma((chunks,)),
            dma((1,)),
            dma((1,)),
            dma((4, 2)),
            dma((2, 2)),
            dma((4, 2)),
            dma((2, 2)),
            dma((3, 3)),
            dma((3,)),
        ],
        compiler_params=pltpu.CompilerParams(
            collective_id=0, has_side_effects=True, vmem_limit_bytes=48 * 2**20
        ),
        cost_estimate=pl.CostEstimate(
            flops=2 * 13 * 4 * tracers.size, bytes_accessed=8 * tracers.size, transcendentals=0
        ),
        name="transport",
    )(*[pltpu.with_memory_space_constraint(a, pltpu.HBM) for a in (tracers, *others)])


def solution(mesh):
    placed = (
        P("tracer", None, "cols", None),
        P(None, "cols", None),
        P(None, "tracer", "cols", None),
        P(None, "tracer", "cols", None),
        P("cols", None),
        P("cols", None),
        P("tracer", "cols", None),
        P("tracer", "cols", None),
    )
    return jax.shard_map(
        functools.partial(on_device, mesh.shape["cols"] // 2),
        mesh=mesh,
        in_specs=placed,
        out_specs=P("tracer", None, "cols", None),
        check_vma=False,
    )
```

```python
import functools

import jax
import jax.numpy as jnp
from jax import lax
from jax.experimental import pallas as pl
from jax.experimental.pallas import tpu as pltpu
from jax.sharding import PartitionSpec as P

SUBSTEPS = 2
max_courant = 0.15
MESH = pl.DeviceIdType.MESH
CHUNK = 8
LAG = 5
FIRST = 2
EARLY = 5
NAHEAD = 5
RESTS = 8
NLAG = 8
AHEAD = 3
SPREAD = 0
WIDTH = 8
HALO = 6


def face_weights(courant, flux):
    speed = jnp.abs(courant)
    half = 0.5 * speed
    bend = 3.0 * half * (1.0 - 2.0 * speed / 3.0)
    centre = flux * (1.0 - half - bend) / 12.0
    upwind = flux * (half - bend) / 12.0
    donor = 2.0 * flux * bend
    east = courant > 0.0
    zero = jnp.zeros_like(courant)
    up_p, up_n = jnp.where(east, upwind, zero), jnp.where(east, zero, upwind)
    don_p, don_n = jnp.where(east, donor, zero), jnp.where(east, zero, donor)
    return (
        -up_p,
        7.0 * up_p - centre,
        7.0 * (up_p + centre) - up_n + don_p,
        7.0 * (up_n + centre) - up_p + don_n,
        7.0 * up_n - centre,
        -up_n,
    )


def cell_weights(faces, shift, mass, new_mass):
    zero = jnp.zeros_like(mass)
    near = faces + (zero,)
    far = (zero,) + tuple(shift(w) for w in faces)
    inverse = 1.0 / new_mass
    out = []
    for j in range(7):
        total = near[j] - far[j]
        if j == 3:
            total = total + mass
        out.append(total * inverse)
    return out


def kernel(
    ring,
    tracers,
    air,
    wind_x,
    wind_y,
    space_x,
    space_y,
    edge_x,
    edge_y,
    out,
    tile,
    halo,
    res,
    fld,
    mine,
    raw,
    kw,
    met,
    load_sem,
    loc_sem,
    pin_s,
    pin_r,
    own_s,
    own_r,
    rel_s,
    rel_r,
    fin_sem,
    out_s,
    out_r,
    rest_s,
    rest_r,
    one_s,
    one_r,
    two_s,
    two_r,
    edge_s,
    edge_r,
    air_s,
    air_r,
):
    count = tracers.shape[0]
    chunks = count // CHUNK
    t = lax.axis_index("tracer")
    c = lax.axis_index("cols")
    core, hi = t % 2, t // 2
    par, s = c % 2, c // 2
    here = 2 * s
    group = (hi + par + 1) % 2
    base = 2 * group
    away = 2 - base
    partner = (t, here + 1 - par)
    up = (t, 2 * ((s + 1) % ring) + par)
    down = (t, 2 * ((s + ring - 1) % ring) + par)
    other = 2 * hi + 1 - core
    across = 2 * (1 - hi) + core
    across_other = 2 * (1 - hi) + 1 - core

    barrier = pltpu.get_barrier_semaphore()

    def enter(device, column):
        pl.semaphore_signal(barrier, inc=1, device_id=(device, column), device_id_type=MESH)

    beside = (2 * ((s + 1) % ring) + 1, 2 * ((s + ring - 1) % ring) + 1)

    @pl.when(par == 1)
    def _():
        enter(*partner)
        enter(other, c)
        for column in beside:
            enter(t, column)
            enter(other, column)

    @pl.when(par == 0)
    def _():
        enter(across, here + 1)
        enter(across_other, here + 1)
        for column in beside:
            enter(t, column)
            enter(across, column)
            enter(across_other, column)

    loads = [
        pltpu.make_async_copy(wind_x.at[0, 0], raw.at[0], load_sem.at[0]),
        pltpu.make_async_copy(wind_x.at[1, 0], raw.at[1], load_sem.at[1]),
        pltpu.make_async_copy(wind_y.at[0, 0], raw.at[2], load_sem.at[2]),
        pltpu.make_async_copy(wind_y.at[1, 0], raw.at[3], load_sem.at[3]),
        pltpu.make_async_copy(space_x, raw.at[4], load_sem.at[4]),
        pltpu.make_async_copy(space_y, raw.at[5], load_sem.at[5]),
        pltpu.make_async_copy(edge_x.at[0], mine.at[4], load_sem.at[6]),
        pltpu.make_async_copy(edge_y.at[0], mine.at[5], load_sem.at[7]),
        pltpu.make_async_copy(
            air.at[pl.ds(base, 2)], fld.at[:, 6, pl.ds(pl.multiple_of(8 + 8 * par, 8), 8)], load_sem.at[8]
        ),
    ]
    for copy in loads:
        copy.start()

    def rows_of(k):
        return pl.ds(pl.multiple_of(k * CHUNK, CHUNK), CHUNK)

    def remote(src, dst, send, recv, k, device):
        return pltpu.make_async_remote_copy(
            src_ref=src,
            dst_ref=dst,
            send_sem=send.at[k],
            recv_sem=recv.at[k],
            device_id=device,
            device_id_type=MESH,
        )

    def local_in():
        return pltpu.make_async_copy(tracers.at[:, pl.ds(base, 2)], tile.at[par], loc_sem.at[0])

    def pair_in(k):
        rows = rows_of(k)
        return remote(tracers.at[rows, pl.ds(away, 2)], tile.at[par, rows], pin_s, pin_r, k, partner)

    own_to_first = (s + ring - 1 + 2 * par) % ring == 0
    relay_to_first = (s + ring + 1 - 2 * par) % ring == 0

    def pair_part(k, rows, start, columns, send, recv):
        part = pl.ds(start, columns)
        return remote(
            tracers.at[rows, pl.ds(away, 2), part], tile.at[par, rows, :, part], send, recv, k, partner
        )

    def pair_edge(k):
        return pair_part(k, rows_of(k), 2 * par, HALO, pin_s, pin_r)

    def pair_rest(n):
        rows = pl.ds(pl.multiple_of(n * RESTS * CHUNK, CHUNK), RESTS * CHUNK)
        return pair_part(n, rows, HALO * (1 - par), 2, rest_s, rest_r)

    def pair_start(k):
        @pl.when(own_to_first)
        def _():
            pair_edge(k).start()

        @pl.when(jnp.logical_not(own_to_first))
        def _():
            pair_in(k).start()

    def own_halo(k):
        rows = rows_of(k)
        return remote(
            tile.at[par, rows, :, pl.ds(2 * par, HALO)],
            halo.at[1 - par, rows, :, pl.ds(0, HALO)],
            own_s,
            own_r,
            k,
            (t, 2 * ((s + ring - 1 + 2 * par) % ring) + par),
        )

    def relay_halo(k):
        rows = rows_of(k)
        return remote(
            tile.at[1 - par, rows, :, pl.ds(2 * (1 - par), HALO)],
            halo.at[par, rows, :, pl.ds(0, HALO)],
            rel_s,
            rel_r,
            k,
            (t, 2 * ((s + ring + 1 - 2 * par) % ring) + par),
        )

    def send_out(k, l):
        rows = rows_of(k)
        return remote(res.at[1 - par, rows, l], out.at[rows, base + l], out_s, out_r, 2 * k + l, partner)

    def keep_out(k):
        rows = rows_of(k)
        return pltpu.make_async_copy(res.at[par, rows], out.at[rows, pl.ds(base, 2)], fin_sem.at[k])

    @pl.when(par == 0)
    def _():
        pl.semaphore_wait(barrier, 1)
        pl.semaphore_signal(met, inc=1, device_id=partner, device_id_type=MESH)

    @pl.when(par == 1)
    def _():
        pl.semaphore_wait(met, 1)

    for k in range(min(FIRST, chunks)):
        pair_start(k)

    for copy in loads:
        copy.wait()
    for direction in range(2):
        for substep in range(SUBSTEPS):
            weight = (2.0 * substep + 1.0) / (2.0 * SUBSTEPS)
            wind = (1.0 - weight) * raw[2 * direction] + weight * raw[2 * direction + 1]
            courant = max_courant * wind * raw[4 + direction]
            if direction == 1:
                row = lax.broadcasted_iota(jnp.int32, courant.shape, 1)
                courant = jnp.where(row > 0, courant, jnp.zeros_like(courant))
            mine[2 * direction + substep] = courant

    @pl.when(par == 1)
    def _():
        fld[core, 0:6, 2 * WIDTH : 3 * WIDTH] = mine[...]

    whole = pl.ds(0, 6)
    west = pl.ds(WIDTH - 3, 3)
    east = pl.ds(3 * WIDTH, 4)
    tiles = (pl.ds(WIDTH, WIDTH), pl.ds(2 * WIDTH, WIDTH))
    even_tile = remote(mine, fld.at[core, whole, tiles[0]], one_s, one_r, 0, partner)
    sweepers = ((t, 1), (other, 1), (across, 0), (across_other, 0))

    def spread(m):
        place = fld.at[core, whole, tiles[m]]
        return [
            remote(place, place, two_s.at[n], two_r.at[core], m, (device, here + p))
            for n, (device, p) in enumerate(sweepers)
            if n > 0
        ]

    def spread_edge(m):
        start, place, column = ((WIDTH, east, down[1]), (3 * WIDTH - 3, west, up[1]))[m]
        return [
            remote(
                fld.at[core, whole, pl.ds(start, place.size)],
                fld.at[core, whole, place],
                edge_s.at[n],
                edge_r.at[core],
                m,
                (device, column - par + p),
            )
            for n, (device, p) in enumerate(sweepers)
        ]

    def spread_wait(slot):
        for m, part in enumerate(tiles):
            place = fld.at[slot, whole, part]
            pltpu.make_async_copy(place, place, two_r.at[slot, m]).wait()

    air_pair = remote(
        air.at[pl.ds(away, 2)],
        fld.at[:, 6, pl.ds(pl.multiple_of(8 + 8 * par, 8), 8)],
        air_s.at[0],
        air_r,
        0,
        partner,
    )

    def air_edges(side, to):
        columns, place = ((pl.ds(0, 4), east), (pl.ds(5, 3), west))[side]
        return [
            remote(
                air.at[pl.ds(2 * ((hi + p + 1) % 2), 2), columns],
                fld.at[:, 6, place],
                air_s.at[p + 1],
                air_r,
                2 - side,
                (t, to - side + p),
            )
            for p in range(2)
        ]

    @pl.when(par == 0)
    def _():
        even_tile.start()

    air_pair.start()
    for k in range(FIRST, min(AHEAD, chunks)):
        pair_start(k)
    local_in().start()

    @pl.when((s == 1) | (s == ring - 1))
    def _():
        for k in range(AHEAD, NAHEAD):
            pair_start(k)

    @pl.when(s == 0)
    def _():
        for k in range(AHEAD, EARLY):
            pair_start(k)

    @pl.when(par == 1)
    def _():
        pl.semaphore_wait(barrier, 13)
        pl.semaphore_signal(met, inc=1, device_id=partner, device_id_type=MESH)
        for copy in spread(1) + spread_edge(1):
            copy.start()

    @pl.when(par == 0)
    def _():
        pl.semaphore_wait(met, 1)

    @pl.when(par == 0)
    def _():
        for copy in air_edges(0, down[1]):
            copy.start()

    @pl.when(par == 1)
    def _():
        for copy in air_edges(1, up[1]):
            copy.start()

    def fields_wait():
        air_pair.wait_recv()
        for slot in range(2):
            for m, part in enumerate((east, west)):
                place = fld.at[slot, whole, part]
                pltpu.make_async_copy(place, place, edge_r.at[slot, m]).wait()
        for side in range(2):
            place = fld.at[:, 6, (east, west)[side]]
            pltpu.make_async_copy(place, place, air_r.at[2 - side]).wait()

        @pl.when(par == 1)
        def _():
            spread_wait(1 - core)

        @pl.when(par == 0)
        def _():
            spread_wait(0)
            spread_wait(1)

    def weights():
        fields_wait()

        def level(l, carry):
            mass = fld[l, 6]
            shape = mass.shape
            row = lax.broadcasted_iota(jnp.int32, shape, 1)
            last = shape[1] - 1
            for sub in range(SUBSTEPS):
                courant_x, courant_y = fld[l, sub], fld[l, 2 + sub]
                flux_x, flux_y = courant_x * fld[l, 4], courant_y * fld[l, 5]

                def next_x(v):
                    return pltpu.roll(v, shape[0] - 1, axis=0)

                def next_y(v):
                    return pltpu.roll(v, shape[1] - 1, axis=1)

                new_mass = mass - (next_x(flux_x) - flux_x)
                kx = cell_weights(face_weights(courant_x, flux_x), next_x, mass, new_mass)
                mass = new_mass
                new_mass = mass - (next_y(flux_y) - flux_y)
                ky = cell_weights(face_weights(courant_y, flux_y), next_y, mass, new_mass)
                mass = new_mass
                for side in (-1, 1):
                    for reach in (3, 2):
                        far, near = 3 + side * reach, 3 + side * (reach - 1)
                        outside = (row < reach) if side < 0 else (row > last - reach)
                        moved = jnp.where(outside, ky[far], 0.0)
                        ky[near] = ky[near] + moved
                        ky[far] = ky[far] - moved
                    far = 3 + side
                    outside = (row < 1) if side < 0 else (row > last - 1)
                    moved = jnp.where(outside, ky[far], 0.0)
                    ky[3] = ky[3] + moved
                    ky[far] = ky[far] - moved
                for j in range(7):
                    kw[l, sub, j] = kx[j]
                kw[l, sub, 7] = ky[3]
                kw[l, sub, 8] = ky[2]
                kw[l, sub, 9] = pltpu.roll(ky[1], shape[1] - 2, axis=1)
                kw[l, sub, 10] = pltpu.roll(ky[0], shape[1] - 2, axis=1)
                kw[l, sub, 11] = pltpu.roll(ky[5], 2, axis=1)
                kw[l, sub, 12] = pltpu.roll(ky[4], 2, axis=1)
                kw[l, sub, 13] = ky[6]
            return carry

        lax.fori_loop(0, 2, level, 0)

    def sweep(l, sub, row, cells):
        def w(j):
            return kw[l, sub, j, pl.ds(row, 1), :]

        x = w(0) * cells[0]
        for j in range(1, 7):
            x = x + w(j) * cells[j]
        lanes = x.shape[1]
        before = pltpu.roll(x, 1, axis=1)
        total = w(7) * x + w(8) * before
        total = total + pltpu.roll(w(9) * x + w(10) * before, 2, axis=1)
        total = total + pltpu.roll(w(11) * x + w(12) * before, lanes - 2, axis=1)
        return total + w(13) * pltpu.roll(x, lanes - 3, axis=1)

    def flat(ref):
        return ref.reshape(3 * count * 2 * WIDTH, ref.shape[-1])

    def compute(k):
        def level(l, carry):
            def column(ref, side, col):
                row = ((side * count + k * CHUNK) * 2 + l) * WIDTH + col
                return flat(ref).at[pl.ds(row, CHUNK, stride=2 * WIDTH), :]

            start = [column(halo, 0, i)[...] for i in range(HALO)]
            start += [column(tile, side, i)[...] for side in range(2) for i in range(WIDTH)]
            start += [column(halo, 1, i)[...] for i in range(HALO)]
            middle = [sweep(l, 0, 5 + i, start[i : i + 7]) for i in range(2 * WIDTH + HALO)]
            for i in range(2 * WIDTH):
                column(res, i // WIDTH, i % WIDTH)[...] = sweep(l, 1, 8 + i, middle[i : i + 7])
            send_out(k, l).start()
            return carry

        lax.fori_loop(0, 2, level, 0)

    next_first = (s == 1) | (s == ring - 1)
    ahead = jnp.where(s > 0, jnp.where(next_first, NAHEAD, AHEAD), EARLY)
    lag = jnp.where(next_first, NLAG, LAG)

    local_in().wait()

    def step(k, carry):
        @pl.when(k < chunks)
        def _():
            @pl.when(relay_to_first)
            def _():
                pair_edge(k).wait_recv()

            @pl.when(jnp.logical_not(relay_to_first))
            def _():
                pair_in(k).wait_recv()

            @pl.when(k + ahead < chunks)
            def _():
                pair_start(k + ahead)

            relay_halo(k).start()


        rest = k - (chunks - NAHEAD)

        @pl.when(own_to_first & (rest >= 0) & (rest < chunks // RESTS))
        def _():
            pair_rest(rest).start()

        @pl.when(2 * k < chunks)
        def _():
            for n in range(2):
                own_halo(2 * k + n).start()

        @pl.when((k == SPREAD) & (par == 1))
        def _():
            even_tile.wait_recv()
            for copy in spread_edge(0) + spread(0):
                copy.start()

        @pl.when(k == lag)
        def _():
            weights()

        @pl.when((k >= lag) & (k < chunks + lag))
        def _():
            done = k - lag

            @pl.when(relay_to_first & (done % RESTS == 0))
            def _():
                pair_rest(done // RESTS).wait_recv()

            own_halo(done).wait_recv()
            relay_halo(done).wait_recv()
            compute(done)
            keep_out(done).start()

        return carry

    lax.fori_loop(0, chunks + max(LAG, NLAG), step, 0)

    air_pair.wait_send()

    @pl.when(par == 0)
    def _():
        even_tile.wait_send()
        for copy in air_edges(0, down[1]):
            copy.wait_send()

    @pl.when(par == 1)
    def _():
        for copy in spread(0) + spread(1) + spread_edge(0) + spread_edge(1) + air_edges(1, up[1]):
            copy.wait_send()

    def sent(k, carry):
        @pl.when(own_to_first)
        def _():
            pair_edge(k).wait_send()

        @pl.when(jnp.logical_not(own_to_first))
        def _():
            pair_in(k).wait_send()

        own_halo(k).wait_send()
        relay_halo(k).wait_send()
        return carry

    lax.fori_loop(0, chunks, sent, 0)

    @pl.when(own_to_first)
    def _():
        for n in range(chunks // RESTS):
            pair_rest(n).wait_send()

    def finish(k, carry):
        keep_out(k).wait()
        for l in range(2):
            send_out(k, l).wait()
        return carry

    lax.fori_loop(0, chunks, finish, 0)


def on_device(ring, tracers, *others):
    count, levels, columns, rows = tracers.shape
    chunks = count // CHUNK
    anywhere = pl.BlockSpec(memory_space=pl.ANY)
    dma = pltpu.SemaphoreType.DMA
    f32 = jnp.float32
    return pl.pallas_call(
        functools.partial(kernel, ring),
        out_shape=pltpu.VMEM(tracers.shape, f32),
        in_specs=[anywhere] * 8,
        out_specs=pl.BlockSpec(memory_space=pltpu.VMEM),
        scratch_shapes=[
            pltpu.VMEM((3, count, 2, WIDTH, rows), f32),
            pltpu.VMEM((3, count, 2, WIDTH, rows), f32),
            pltpu.VMEM((3, count, 2, WIDTH, rows), f32),
            pltpu.VMEM((2, 7, 4 * WIDTH, rows), f32),
            pltpu.VMEM((6, WIDTH, rows), f32),
            pltpu.VMEM((6, WIDTH, rows), f32),
            pltpu.VMEM((2, SUBSTEPS, 14, 4 * WIDTH, rows), f32),
            pltpu.SemaphoreType.REGULAR,
            dma((9,)),
            dma((chunks,)),
            dma((chunks,)),
            dma((chunks,)),
            dma((chunks,)),
            dma((chunks,)),
            dma((chunks,)),
            dma((chunks,)),
            dma((chunks,)),
            dma((2 * chunks,)),
            dma((2 * chunks,)),
            dma((chunks,)),
            dma((chunks,)),
            dma((1,)),
            dma((1,)),
            dma((4, 2)),
            dma((2, 2)),
            dma((4, 2)),
            dma((2, 2)),
            dma((3, 3)),
            dma((3,)),
        ],
        compiler_params=pltpu.CompilerParams(
            collective_id=0, has_side_effects=True, vmem_limit_bytes=48 * 2**20
        ),
        cost_estimate=pl.CostEstimate(
            flops=2 * 13 * 4 * tracers.size, bytes_accessed=8 * tracers.size, transcendentals=0
        ),
        name="transport",
    )(*[pltpu.with_memory_space_constraint(a, pltpu.HBM) for a in (tracers, *others)])


def solution(mesh):
    placed = (
        P("tracer", None, "cols", None),
        P(None, "cols", None),
        P(None, "tracer", "cols", None),
        P(None, "tracer", "cols", None),
        P("cols", None),
        P("cols", None),
        P("tracer", "cols", None),
        P("tracer", "cols", None),
    )
    return jax.shard_map(
        functools.partial(on_device, mesh.shape["cols"] // 2),
        mesh=mesh,
        in_specs=placed,
        out_specs=P("tracer", None, "cols", None),
        check_vma=False,
    )
```

```python
import functools

import jax
import jax.numpy as jnp
from jax import lax
from jax.experimental import pallas as pl
from jax.experimental.pallas import tpu as pltpu
from jax.sharding import PartitionSpec as P

SUBSTEPS = 2
max_courant = 0.15
MESH = pl.DeviceIdType.MESH
CHUNK = 8
LAG = 6
FIRST = 2
EARLY = 5
NAHEAD = 5
RESTS = 8
NLAG = 8
AHEAD = 3
SPREAD = 0
WIDTH = 8
HALO = 6


def face_weights(courant, flux):
    speed = jnp.abs(courant)
    half = 0.5 * speed
    bend = 3.0 * half * (1.0 - 2.0 * speed / 3.0)
    centre = flux * (1.0 - half - bend) / 12.0
    upwind = flux * (half - bend) / 12.0
    donor = 2.0 * flux * bend
    east = courant > 0.0
    zero = jnp.zeros_like(courant)
    up_p, up_n = jnp.where(east, upwind, zero), jnp.where(east, zero, upwind)
    don_p, don_n = jnp.where(east, donor, zero), jnp.where(east, zero, donor)
    return (
        -up_p,
        7.0 * up_p - centre,
        7.0 * (up_p + centre) - up_n + don_p,
        7.0 * (up_n + centre) - up_p + don_n,
        7.0 * up_n - centre,
        -up_n,
    )


def cell_weights(faces, shift, mass, new_mass):
    zero = jnp.zeros_like(mass)
    near = faces + (zero,)
    far = (zero,) + tuple(shift(w) for w in faces)
    inverse = 1.0 / new_mass
    out = []
    for j in range(7):
        total = near[j] - far[j]
        if j == 3:
            total = total + mass
        out.append(total * inverse)
    return out


def kernel(
    ring,
    tracers,
    air,
    wind_x,
    wind_y,
    space_x,
    space_y,
    edge_x,
    edge_y,
    out,
    tile,
    halo,
    res,
    fld,
    mine,
    raw,
    kw,
    met,
    load_sem,
    loc_sem,
    pin_s,
    pin_r,
    own_s,
    own_r,
    rel_s,
    rel_r,
    fin_sem,
    out_s,
    out_r,
    rest_s,
    rest_r,
    one_s,
    one_r,
    two_s,
    two_r,
    edge_s,
    edge_r,
    air_s,
    air_r,
):
    count = tracers.shape[0]
    chunks = count // CHUNK
    t = lax.axis_index("tracer")
    c = lax.axis_index("cols")
    core, hi = t % 2, t // 2
    par, s = c % 2, c // 2
    here = 2 * s
    group = (hi + par + 1) % 2
    base = 2 * group
    away = 2 - base
    partner = (t, here + 1 - par)
    up = (t, 2 * ((s + 1) % ring) + par)
    down = (t, 2 * ((s + ring - 1) % ring) + par)
    other = 2 * hi + 1 - core
    across = 2 * (1 - hi) + core
    across_other = 2 * (1 - hi) + 1 - core

    barrier = pltpu.get_barrier_semaphore()

    def enter(device, column):
        pl.semaphore_signal(barrier, inc=1, device_id=(device, column), device_id_type=MESH)

    beside = (2 * ((s + 1) % ring) + 1, 2 * ((s + ring - 1) % ring) + 1)

    @pl.when(par == 1)
    def _():
        enter(*partner)
        enter(other, c)
        for column in beside:
            enter(t, column)
            enter(other, column)

    @pl.when(par == 0)
    def _():
        enter(across, here + 1)
        enter(across_other, here + 1)
        for column in beside:
            enter(t, column)
            enter(across, column)
            enter(across_other, column)

    loads = [
        pltpu.make_async_copy(wind_x.at[0, 0], raw.at[0], load_sem.at[0]),
        pltpu.make_async_copy(wind_x.at[1, 0], raw.at[1], load_sem.at[1]),
        pltpu.make_async_copy(wind_y.at[0, 0], raw.at[2], load_sem.at[2]),
        pltpu.make_async_copy(wind_y.at[1, 0], raw.at[3], load_sem.at[3]),
        pltpu.make_async_copy(space_x, raw.at[4], load_sem.at[4]),
        pltpu.make_async_copy(space_y, raw.at[5], load_sem.at[5]),
        pltpu.make_async_copy(edge_x.at[0], mine.at[4], load_sem.at[6]),
        pltpu.make_async_copy(edge_y.at[0], mine.at[5], load_sem.at[7]),
        pltpu.make_async_copy(
            air.at[pl.ds(base, 2)], fld.at[:, 6, pl.ds(pl.multiple_of(8 + 8 * par, 8), 8)], load_sem.at[8]
        ),
    ]
    for copy in loads:
        copy.start()

    def rows_of(k):
        return pl.ds(pl.multiple_of(k * CHUNK, CHUNK), CHUNK)

    def remote(src, dst, send, recv, k, device):
        return pltpu.make_async_remote_copy(
            src_ref=src,
            dst_ref=dst,
            send_sem=send.at[k],
            recv_sem=recv.at[k],
            device_id=device,
            device_id_type=MESH,
        )

    def local_in():
        return pltpu.make_async_copy(tracers.at[:, pl.ds(base, 2)], tile.at[par], loc_sem.at[0])

    def pair_in(k):
        rows = rows_of(k)
        return remote(tracers.at[rows, pl.ds(away, 2)], tile.at[par, rows], pin_s, pin_r, k, partner)

    own_to_first = (s + ring - 1 + 2 * par) % ring == 0
    relay_to_first = (s + ring + 1 - 2 * par) % ring == 0

    def pair_part(k, rows, start, columns, send, recv):
        part = pl.ds(start, columns)
        return remote(
            tracers.at[rows, pl.ds(away, 2), part], tile.at[par, rows, :, part], send, recv, k, partner
        )

    def pair_edge(k):
        return pair_part(k, rows_of(k), 2 * par, HALO, pin_s, pin_r)

    def pair_rest(n):
        rows = pl.ds(pl.multiple_of(n * RESTS * CHUNK, CHUNK), RESTS * CHUNK)
        return pair_part(n, rows, HALO * (1 - par), 2, rest_s, rest_r)

    def pair_start(k):
        @pl.when(own_to_first)
        def _():
            pair_edge(k).start()

        @pl.when(jnp.logical_not(own_to_first))
        def _():
            pair_in(k).start()

    def own_halo(k):
        rows = rows_of(k)
        return remote(
            tile.at[par, rows, :, pl.ds(2 * par, HALO)],
            halo.at[1 - par, rows, :, pl.ds(0, HALO)],
            own_s,
            own_r,
            k,
            (t, 2 * ((s + ring - 1 + 2 * par) % ring) + par),
        )

    def relay_halo(k):
        rows = rows_of(k)
        return remote(
            tile.at[1 - par, rows, :, pl.ds(2 * (1 - par), HALO)],
            halo.at[par, rows, :, pl.ds(0, HALO)],
            rel_s,
            rel_r,
            k,
            (t, 2 * ((s + ring + 1 - 2 * par) % ring) + par),
        )

    def send_out(k, l):
        rows = rows_of(k)
        return remote(res.at[1 - par, rows, l], out.at[rows, base + l], out_s, out_r, 2 * k + l, partner)

    def keep_out(k):
        rows = rows_of(k)
        return pltpu.make_async_copy(res.at[par, rows], out.at[rows, pl.ds(base, 2)], fin_sem.at[k])

    @pl.when(par == 0)
    def _():
        pl.semaphore_wait(barrier, 1)
        pl.semaphore_signal(met, inc=1, device_id=partner, device_id_type=MESH)

    @pl.when(par == 1)
    def _():
        pl.semaphore_wait(met, 1)

    for k in range(min(FIRST, chunks)):
        pair_start(k)

    for copy in loads:
        copy.wait()
    for direction in range(2):
        for substep in range(SUBSTEPS):
            weight = (2.0 * substep + 1.0) / (2.0 * SUBSTEPS)
            wind = (1.0 - weight) * raw[2 * direction] + weight * raw[2 * direction + 1]
            courant = max_courant * wind * raw[4 + direction]
            if direction == 1:
                row = lax.broadcasted_iota(jnp.int32, courant.shape, 1)
                courant = jnp.where(row > 0, courant, jnp.zeros_like(courant))
            mine[2 * direction + substep] = courant

    @pl.when(par == 1)
    def _():
        fld[core, 0:6, 2 * WIDTH : 3 * WIDTH] = mine[...]

    whole = pl.ds(0, 6)
    west = pl.ds(WIDTH - 3, 3)
    east = pl.ds(3 * WIDTH, 4)
    tiles = (pl.ds(WIDTH, WIDTH), pl.ds(2 * WIDTH, WIDTH))
    even_tile = remote(mine, fld.at[core, whole, tiles[0]], one_s, one_r, 0, partner)
    sweepers = ((t, 1), (other, 1), (across, 0), (across_other, 0))

    def spread(m):
        place = fld.at[core, whole, tiles[m]]
        return [
            remote(place, place, two_s.at[n], two_r.at[core], m, (device, here + p))
            for n, (device, p) in enumerate(sweepers)
            if n > 0
        ]

    def spread_edge(m):
        start, place, column = ((WIDTH, east, down[1]), (3 * WIDTH - 3, west, up[1]))[m]
        return [
            remote(
                fld.at[core, whole, pl.ds(start, place.size)],
                fld.at[core, whole, place],
                edge_s.at[n],
                edge_r.at[core],
                m,
                (device, column - par + p),
            )
            for n, (device, p) in enumerate(sweepers)
        ]

    def spread_wait(slot):
        for m, part in enumerate(tiles):
            place = fld.at[slot, whole, part]
            pltpu.make_async_copy(place, place, two_r.at[slot, m]).wait()

    air_pair = remote(
        air.at[pl.ds(away, 2)],
        fld.at[:, 6, pl.ds(pl.multiple_of(8 + 8 * par, 8), 8)],
        air_s.at[0],
        air_r,
        0,
        partner,
    )

    def air_edges(side, to):
        columns, place = ((pl.ds(0, 4), east), (pl.ds(5, 3), west))[side]
        return [
            remote(
                air.at[pl.ds(2 * ((hi + p + 1) % 2), 2), columns],
                fld.at[:, 6, place],
                air_s.at[p + 1],
                air_r,
                2 - side,
                (t, to - side + p),
            )
            for p in range(2)
        ]

    @pl.when(par == 0)
    def _():
        even_tile.start()

    air_pair.start()
    for k in range(FIRST, min(AHEAD, chunks)):
        pair_start(k)
    local_in().start()

    @pl.when((s == 1) | (s == ring - 1))
    def _():
        for k in range(AHEAD, NAHEAD):
            pair_start(k)

    @pl.when(s == 0)
    def _():
        for k in range(AHEAD, EARLY):
            pair_start(k)

    @pl.when(par == 1)
    def _():
        pl.semaphore_wait(barrier, 13)
        pl.semaphore_signal(met, inc=1, device_id=partner, device_id_type=MESH)
        for copy in spread(1) + spread_edge(1):
            copy.start()

    @pl.when(par == 0)
    def _():
        pl.semaphore_wait(met, 1)

    @pl.when(par == 0)
    def _():
        for copy in air_edges(0, down[1]):
            copy.start()

    @pl.when(par == 1)
    def _():
        for copy in air_edges(1, up[1]):
            copy.start()

    def fields_wait():
        air_pair.wait_recv()
        for slot in range(2):
            for m, part in enumerate((east, west)):
                place = fld.at[slot, whole, part]
                pltpu.make_async_copy(place, place, edge_r.at[slot, m]).wait()
        for side in range(2):
            place = fld.at[:, 6, (east, west)[side]]
            pltpu.make_async_copy(place, place, air_r.at[2 - side]).wait()

        @pl.when(par == 1)
        def _():
            spread_wait(1 - core)

        @pl.when(par == 0)
        def _():
            spread_wait(0)
            spread_wait(1)

    def weights():
        fields_wait()

        def level(l, carry):
            mass = fld[l, 6]
            shape = mass.shape
            row = lax.broadcasted_iota(jnp.int32, shape, 1)
            last = shape[1] - 1
            for sub in range(SUBSTEPS):
                courant_x, courant_y = fld[l, sub], fld[l, 2 + sub]
                flux_x, flux_y = courant_x * fld[l, 4], courant_y * fld[l, 5]

                def next_x(v):
                    return pltpu.roll(v, shape[0] - 1, axis=0)

                def next_y(v):
                    return pltpu.roll(v, shape[1] - 1, axis=1)

                new_mass = mass - (next_x(flux_x) - flux_x)
                kx = cell_weights(face_weights(courant_x, flux_x), next_x, mass, new_mass)
                mass = new_mass
                new_mass = mass - (next_y(flux_y) - flux_y)
                ky = cell_weights(face_weights(courant_y, flux_y), next_y, mass, new_mass)
                mass = new_mass
                for side in (-1, 1):
                    for reach in (3, 2):
                        far, near = 3 + side * reach, 3 + side * (reach - 1)
                        outside = (row < reach) if side < 0 else (row > last - reach)
                        moved = jnp.where(outside, ky[far], 0.0)
                        ky[near] = ky[near] + moved
                        ky[far] = ky[far] - moved
                    far = 3 + side
                    outside = (row < 1) if side < 0 else (row > last - 1)
                    moved = jnp.where(outside, ky[far], 0.0)
                    ky[3] = ky[3] + moved
                    ky[far] = ky[far] - moved
                for j in range(7):
                    kw[l, sub, j] = kx[j]
                kw[l, sub, 7] = ky[3]
                kw[l, sub, 8] = ky[2]
                kw[l, sub, 9] = pltpu.roll(ky[1], shape[1] - 2, axis=1)
                kw[l, sub, 10] = pltpu.roll(ky[0], shape[1] - 2, axis=1)
                kw[l, sub, 11] = pltpu.roll(ky[5], 2, axis=1)
                kw[l, sub, 12] = pltpu.roll(ky[4], 2, axis=1)
                kw[l, sub, 13] = ky[6]
            return carry

        lax.fori_loop(0, 2, level, 0)

    def sweep(l, sub, row, cells):
        def w(j):
            return kw[l, sub, j, pl.ds(row, 1), :]

        x = w(0) * cells[0]
        for j in range(1, 7):
            x = x + w(j) * cells[j]
        lanes = x.shape[1]
        before = pltpu.roll(x, 1, axis=1)
        total = w(7) * x + w(8) * before
        total = total + pltpu.roll(w(9) * x + w(10) * before, 2, axis=1)
        total = total + pltpu.roll(w(11) * x + w(12) * before, lanes - 2, axis=1)
        return total + w(13) * pltpu.roll(x, lanes - 3, axis=1)

    def flat(ref):
        return ref.reshape(3 * count * 2 * WIDTH, ref.shape[-1])

    def compute(k):
        def level(l, carry):
            def column(ref, side, col):
                row = ((side * count + k * CHUNK) * 2 + l) * WIDTH + col
                return flat(ref).at[pl.ds(row, CHUNK, stride=2 * WIDTH), :]

            start = [column(halo, 0, i)[...] for i in range(HALO)]
            start += [column(tile, side, i)[...] for side in range(2) for i in range(WIDTH)]
            start += [column(halo, 1, i)[...] for i in range(HALO)]
            middle = [sweep(l, 0, 5 + i, start[i : i + 7]) for i in range(2 * WIDTH + HALO)]
            for i in range(2 * WIDTH):
                column(res, i // WIDTH, i % WIDTH)[...] = sweep(l, 1, 8 + i, middle[i : i + 7])
            send_out(k, l).start()
            return carry

        lax.fori_loop(0, 2, level, 0)

    next_first = (s == 1) | (s == ring - 1)
    ahead = jnp.where(s > 0, jnp.where(next_first, NAHEAD, AHEAD), EARLY)
    lag = jnp.where(next_first, NLAG, LAG)

    local_in().wait()

    def step(k, carry):
        @pl.when(k < chunks)
        def _():
            @pl.when(relay_to_first)
            def _():
                pair_edge(k).wait_recv()

            @pl.when(jnp.logical_not(relay_to_first))
            def _():
                pair_in(k).wait_recv()

            @pl.when(k + ahead < chunks)
            def _():
                pair_start(k + ahead)

            relay_halo(k).start()


        rest = k - (chunks - NAHEAD)

        @pl.when(own_to_first & (rest >= 0) & (rest < chunks // RESTS))
        def _():
            pair_rest(rest).start()

        @pl.when(2 * k < chunks)
        def _():
            for n in range(2):
                own_halo(2 * k + n).start()

        @pl.when((k == SPREAD) & (par == 1))
        def _():
            even_tile.wait_recv()
            for copy in spread_edge(0) + spread(0):
                copy.start()

        @pl.when(k == lag)
        def _():
            weights()

        @pl.when((k >= lag) & (k < chunks + lag))
        def _():
            done = k - lag

            @pl.when(relay_to_first & (done % RESTS == 0))
            def _():
                pair_rest(done // RESTS).wait_recv()

            own_halo(done).wait_recv()
            relay_halo(done).wait_recv()
            compute(done)
            keep_out(done).start()

        return carry

    lax.fori_loop(0, chunks + max(LAG, NLAG), step, 0)

    air_pair.wait_send()

    @pl.when(par == 0)
    def _():
        even_tile.wait_send()
        for copy in air_edges(0, down[1]):
            copy.wait_send()

    @pl.when(par == 1)
    def _():
        for copy in spread(0) + spread(1) + spread_edge(0) + spread_edge(1) + air_edges(1, up[1]):
            copy.wait_send()

    def sent(k, carry):
        @pl.when(own_to_first)
        def _():
            pair_edge(k).wait_send()

        @pl.when(jnp.logical_not(own_to_first))
        def _():
            pair_in(k).wait_send()

        own_halo(k).wait_send()
        relay_halo(k).wait_send()
        return carry

    lax.fori_loop(0, chunks, sent, 0)

    @pl.when(own_to_first)
    def _():
        for n in range(chunks // RESTS):
            pair_rest(n).wait_send()

    def finish(k, carry):
        keep_out(k).wait()
        for l in range(2):
            send_out(k, l).wait()
        return carry

    lax.fori_loop(0, chunks, finish, 0)


def on_device(ring, tracers, *others):
    count, levels, columns, rows = tracers.shape
    chunks = count // CHUNK
    anywhere = pl.BlockSpec(memory_space=pl.ANY)
    dma = pltpu.SemaphoreType.DMA
    f32 = jnp.float32
    return pl.pallas_call(
        functools.partial(kernel, ring),
        out_shape=pltpu.VMEM(tracers.shape, f32),
        in_specs=[anywhere] * 8,
        out_specs=pl.BlockSpec(memory_space=pltpu.VMEM),
        scratch_shapes=[
            pltpu.VMEM((3, count, 2, WIDTH, rows), f32),
            pltpu.VMEM((3, count, 2, WIDTH, rows), f32),
            pltpu.VMEM((3, count, 2, WIDTH, rows), f32),
            pltpu.VMEM((2, 7, 4 * WIDTH, rows), f32),
            pltpu.VMEM((6, WIDTH, rows), f32),
            pltpu.VMEM((6, WIDTH, rows), f32),
            pltpu.VMEM((2, SUBSTEPS, 14, 4 * WIDTH, rows), f32),
            pltpu.SemaphoreType.REGULAR,
            dma((9,)),
            dma((chunks,)),
            dma((chunks,)),
            dma((chunks,)),
            dma((chunks,)),
            dma((chunks,)),
            dma((chunks,)),
            dma((chunks,)),
            dma((chunks,)),
            dma((2 * chunks,)),
            dma((2 * chunks,)),
            dma((chunks,)),
            dma((chunks,)),
            dma((1,)),
            dma((1,)),
            dma((4, 2)),
            dma((2, 2)),
            dma((4, 2)),
            dma((2, 2)),
            dma((3, 3)),
            dma((3,)),
        ],
        compiler_params=pltpu.CompilerParams(
            collective_id=0, has_side_effects=True, vmem_limit_bytes=48 * 2**20
        ),
        cost_estimate=pl.CostEstimate(
            flops=2 * 13 * 4 * tracers.size, bytes_accessed=8 * tracers.size, transcendentals=0
        ),
        name="transport",
    )(*[pltpu.with_memory_space_constraint(a, pltpu.HBM) for a in (tracers, *others)])


def solution(mesh):
    placed = (
        P("tracer", None, "cols", None),
        P(None, "cols", None),
        P(None, "tracer", "cols", None),
        P(None, "tracer", "cols", None),
        P("cols", None),
        P("cols", None),
        P("tracer", "cols", None),
        P("tracer", "cols", None),
    )
    return jax.shard_map(
        functools.partial(on_device, mesh.shape["cols"] // 2),
        mesh=mesh,
        in_specs=placed,
        out_specs=P("tracer", None, "cols", None),
        check_vma=False,
    )
```
